32 devices in a mesh: dp: 8 (over y, x, core), seq: 4 (over z).
Axes of the slice: x: 2, y: 2, z: 4, core: 2. Of those that a mesh axis runs over, the one named last changes fastest.
Arguments:
- tokens: bfloat16 [4096, 2048], P(('dp', 'seq')), may hold values from -6 to 6
- cotangent: bfloat16 [4096, 2048], P(('dp', 'seq')), may hold values from -6 to 6
- lengths: int32 [8, 8], P('dp'), may hold values from 1 to 448, 512 in all within a row
- norm_attn: float32 [2048], replicated, may hold values from 0.1 to 1.9
- w_query: bfloat16 [2048, 2048], P(('dp', 'seq')), may hold values from -0.125 to 0.125
- w_key: bfloat16 [2048, 2048], P(('dp', 'seq')), may hold values from -0.125 to 0.125
- w_value: bfloat16 [2048, 2048], P(('dp', 'seq')), may hold values from -0.125 to 0.125
- w_out: bfloat16 [2048, 2048], P(('dp', 'seq')), may hold values from -1 to 1
- norm_ffn: float32 [2048], replicated, may hold values from 0.1 to 1.9
- w_gate: bfloat16 [2048, 5632], P(('dp', 'seq')), may hold values from -0.125 to 0.125
- w_up: bfloat16 [2048, 5632], P(('dp', 'seq')), may hold values from -0.125 to 0.125
- w_down: bfloat16 [5632, 2048], P(('dp', 'seq')), may hold values from -0.078125 to 0.078125
Outputs:
- activations: bfloat16 [4096, 2048], P(('dp', 'seq'))
- token_grad: float32 [4096, 2048], P(('dp', 'seq'))
- grad_norm_attn: float32 [2048], replicated
- grad_w_query: float32 [2048, 2048], P(('dp', 'seq'))
- grad_w_key: float32 [2048, 2048], P(('dp', 'seq'))
- grad_w_value: float32 [2048, 2048], P(('dp', 'seq'))
- grad_w_out: float32 [2048, 2048], P(('dp', 'seq'))
- grad_norm_ffn: float32 [2048], replicated
- grad_w_gate: float32 [2048, 5632], P(('dp', 'seq'))
- grad_w_up: float32 [2048, 5632], P(('dp', 'seq'))
- grad_w_down: float32 [5632, 2048], P(('dp', 'seq'))
The draws below stay inside these ranges and needn't reach their ends.
Inputs may be any that keep to these rules, and one draw needn't show every extreme that they name: Each row's lengths add up to 512, and in every row one document is 448 long.
All inputs are finite; a program needn't handle non-finite values.
Results may differ from the reference program's by a relative error of at most 0.014.
Values may be sent and summed in bfloat16 or wider, within the bound.
No kernel may reach another device: no remote copies, remote signals or barrier semaphores. Data moves between devices by JAX's collectives and lax.ppermute only.
A program may use at most 512 MiB of HBM per device.

```python
import math
import jax
import jax.numpy as jnp
import numpy as np
from jax import lax

D = 2048
HEADS = 16
HEAD = 128
FF = 5632
WINDOW = 64
DOCS = 8
ROWS = 8
LENGTH = 512
LONGEST = 448
TOKENS = 4096


def levels(stream_key, shape, shards, low, top_value):
    level, own = 1.0, jax.random.fold_in(stream_key, 6)
    for axis_at, shards_of in shards:
        steps = jnp.exp(jax.random.uniform(jax.random.fold_in(own, axis_at), (shards_of,), jnp.float32, low / len(shards), top_value / len(shards)))
        level = level * jnp.repeat(steps, shape[axis_at] // shards_of).reshape([-1 if axis == axis_at else 1 for axis in range(len(shape))])
    return level


def profile(number_of, total, limit, slope):
    loads = [(1 << 20) // math.isqrt(standing ** slope) + 1 for standing in range(2, number_of + 1)]
    surplus, given = total - limit - (number_of - 1), [1] * (number_of - 1)
    while surplus > 0:
        movable = [i for i in range(number_of - 1) if given[i] < limit]
        pool, remaining = sum([loads[i] for i in movable]), surplus
        for i in movable:
            more = min(limit - given[i], max(1, remaining * loads[i] // pool), surplus)
            given[i] = given[i] + more
            surplus = surplus - more
    return np.array([limit] + given)


def ragged_sizes(key, count, total, most, skew):
    if count == 2:
        one = jax.random.randint(key, (), max(1, total - most), min(most, total - 1) + 1)
        return jnp.stack([one, total - one])
    sizes = jnp.asarray(profile(count, total, most, skew), jnp.int32)
    couples = (count - 1) // 2
    source_of, taker = sizes[1:1 + 2 * couples:2], sizes[2:2 + 2 * couples:2]
    margin = jnp.minimum(source_of - 1, most - taker)
    moved = jax.random.randint(jax.random.fold_in(key, 1), (couples,), 0, 1 << 20) % (margin + 1)
    sizes = sizes.at[1:1 + 2 * couples:2].set(source_of - moved).at[2:2 + 2 * couples:2].set(taker + moved)
    return sizes[jax.random.permutation(jax.random.fold_in(key, 2), count)]


def scatter_about(own_key, shape, width, limit, cuts=(), kind=jnp.bfloat16):
    loudness = levels(own_key, shape, cuts, -0.22, 0.18) if cuts else 1.0
    values = jax.random.normal(own_key, shape, jnp.float32) * width * loudness
    return jnp.minimum(jnp.maximum(values, -limit), limit).astype(kind)


def setup_inputs(seed: int = 0) -> dict:
    streams_of = jax.random.split(jax.random.key(seed), 13)
    tokens = scatter_about(streams_of[0], (TOKENS, D), 1.0, 6.0, ((0, 32),))
    cotangent = scatter_about(streams_of[1], (TOKENS, D), 1.0, 6.0, ((0, 32),))
    lengths = jax.vmap(lambda own: ragged_sizes(own, DOCS, LENGTH, LONGEST, 2))(jax.random.split(streams_of[2], ROWS)).reshape((ROWS, DOCS)).astype(jnp.int32)
    norm_attn = jnp.clip(1.0 + 0.18 * jax.random.normal(streams_of[3], (D,), jnp.float32), 0.1, 1.9)
    w_query = scatter_about(streams_of[4], (D, D), D ** -0.5, 0.125, ((0, 32),))
    w_key = scatter_about(streams_of[5], (D, D), D ** -0.5, 0.125, ((0, 32),))
    w_value = scatter_about(streams_of[6], (D, D), D ** -0.5, 0.125, ((0, 32),))
    w_out = scatter_about(streams_of[7], (D, D), (D // WINDOW) ** -0.5, 1.0, ((0, 32),))
    norm_ffn = jnp.clip(1.0 + 0.18 * jax.random.normal(streams_of[8], (D,), jnp.float32), 0.1, 1.9)
    w_gate = scatter_about(streams_of[9], (D, FF), D ** -0.5, 0.125, ((0, 32),))
    w_up = scatter_about(streams_of[10], (D, FF), D ** -0.5, 0.125, ((0, 32),))
    w_down = scatter_about(streams_of[11], (FF, D), FF ** -0.5, 0.078125, ((0, 32),))
    return {"tokens": tokens, "cotangent": cotangent, "lengths": lengths, "norm_attn": norm_attn, "w_query": w_query, "w_key": w_key, "w_value": w_value, "w_out": w_out, "norm_ffn": norm_ffn, "w_gate": w_gate, "w_up": w_up, "w_down": w_down}


@jax.custom_vjp
def low(v):
    return lax.optimization_barrier(v.astype(jnp.bfloat16)).astype(jnp.float32)

@jax.custom_vjp
def low_back(v):
    return v

def low_keep(v):
    return (low(v), None)

def low_pass(kept, grad):
    return (grad,)

def back_keep(v):
    return (v, None)

def back_low(kept, grad):
    return (low(grad),)
low.defvjp(low_keep, low_pass)
low_back.defvjp(back_keep, back_low)
norm_eps = 1e-05
masked_score = -1e+30
highest = lax.Precision.HIGHEST

def both_ways(values):
    return low_back(low(values))

def product(left, right):
    return jnp.dot(left, right, preferred_element_type=jnp.float32, precision=highest)

def doc_number(positions, doc_ends):
    counted = lax.optimization_barrier(jnp.sum((positions[:, None] >= doc_ends[None, :]).astype(jnp.int32), axis=1))
    return jnp.where(positions < 0, -1, counted).astype(jnp.int32)

def band_window(values, blocks, extent):
    shaped = values.reshape((blocks + 1, extent) + values.shape[1:])
    return jnp.concatenate([shaped[:-1], shaped[1:]], axis=1)

def allowed_pairs(doc_query, doc_keys, blocks, extent):
    offset_query = jnp.arange(extent)[:, None]
    offset_key = jnp.arange(2 * extent)[None, :]
    causal_band = (offset_key > offset_query) & (offset_key <= offset_query + extent)
    same_doc = doc_query.reshape(blocks, extent)[:, :, None] == band_window(doc_keys, blocks, extent)[:, None, :]
    return (causal_band[None] & same_doc)[:, None]

def row_forward(row_tokens, doc_ids, params):
    norm_attn, w_query, w_key, w_value, w_out, norm_ffn, w_gate, w_up, w_down = params
    length = row_tokens.shape[0]
    blocks = length // WINDOW
    score_scale = 1.0 / math.sqrt(HEAD)
    inverse_attn = lax.rsqrt(lax.optimization_barrier(jnp.mean(row_tokens * row_tokens, axis=1, keepdims=True)) + norm_eps)
    normed_attn = low(row_tokens * inverse_attn * norm_attn)
    query = both_ways(product(normed_attn, w_query))
    key_proj = both_ways(product(normed_attn, w_key))
    value_proj = both_ways(product(normed_attn, w_value))
    padding = jnp.zeros((WINDOW, D), jnp.float32)
    key_window = band_window(jnp.concatenate([padding, key_proj], axis=0), blocks, WINDOW).reshape(blocks, 2 * WINDOW, HEADS, HEAD)
    value_window = band_window(jnp.concatenate([padding, value_proj], axis=0), blocks, WINDOW).reshape(blocks, 2 * WINDOW, HEADS, HEAD)
    doc_keys = jnp.concatenate([jnp.full((WINDOW,), -1, jnp.int32), doc_ids])
    allowed = allowed_pairs(doc_ids, doc_keys, blocks, WINDOW)
    query_blocks = query.reshape(blocks, WINDOW, HEADS, HEAD)
    raw = jnp.einsum('bqhd,bkhd->bhqk', query_blocks, key_window, precision=highest) * score_scale
    scores = low_back(raw)
    probs = low(jax.nn.softmax(jnp.where(allowed, scores, masked_score), axis=-1))
    mixed = jnp.einsum('bhqk,bkhd->bqhd', probs, value_window, precision=highest).reshape(length, D)
    attended = both_ways(mixed)
    middle = row_tokens + low_back(product(attended, w_out))
    inverse_ffn = lax.rsqrt(lax.optimization_barrier(jnp.mean(middle * middle, axis=1, keepdims=True)) + norm_eps)
    normed_ffn = low(middle * inverse_ffn * norm_ffn)
    gate = low_back(product(normed_ffn, w_gate))
    up_proj = low_back(product(normed_ffn, w_up))
    hidden = low(jax.nn.silu(gate) * up_proj)
    return middle + low_back(product(hidden, w_down))

def reference(tokens, cotangent, lengths, norm_attn, w_query, w_key, w_value, w_out, norm_ffn, w_gate, w_up, w_down):
    weights = tuple((item.astype(jnp.float32) for item in (norm_attn, w_query, w_key, w_value, w_out, norm_ffn, w_gate, w_up, w_down)))
    row_inputs = tokens.astype(jnp.float32).reshape(ROWS, LENGTH, D)
    row_cotangents = cotangent.astype(jnp.float32).reshape(ROWS, LENGTH, D)
    positions = jnp.arange(LENGTH, dtype=jnp.int32)

    def one_row(totals, inputs):
        row_tokens, row_cotangent, row_lengths = inputs
        doc_ids = doc_number(positions, jnp.cumsum(row_lengths).astype(jnp.int32))

        def forward(values, params):
            return row_forward(values, doc_ids, params)
        result, pullback = jax.vjp(forward, row_tokens, weights)
        input_grad, weight_grads = pullback(row_cotangent)
        totals = jax.tree.map(jnp.add, totals, weight_grads)
        return (totals, (result.astype(jnp.bfloat16), input_grad))
    initial = jax.tree.map(jnp.zeros_like, weights)
    totals, outputs = lax.scan(one_row, initial, (row_inputs, row_cotangents, lengths))
    activations = outputs[0].reshape(TOKENS, D)
    token_grad = outputs[1].reshape(TOKENS, D)
    return (activations, token_grad, totals[0], totals[1], totals[2], totals[3], totals[4], totals[5], totals[6], totals[7], totals[8])
```

```python
import math

import jax
import jax.numpy as jnp
from jax import lax
from jax.sharding import Mesh
from jax.sharding import PartitionSpec as P

HEADS = 16
HEAD = 128
WINDOW = 64

ALL = ("y", "x", "c", "z")
norm_eps = 1e-05
masked_score = -1e30
f32 = jnp.float32
bf16 = jnp.bfloat16


def dot(left, right, dims=((1,), (0,))):
    return lax.dot_general(left, right, (dims, ((), ())), preferred_element_type=f32)


def dot_nt(left, right):
    return dot(left, right, ((1,), (1,)))


def dot_tn(left, right):
    return dot(left, right, ((0,), (0,)))


def swap(x, axis):
    return lax.ppermute(x, axis, [(0, 1), (1, 0)])


def ring_order(n):
    return list(range(1, n, 2)) + list(range(n - 2, -1, -2)) if n > 1 else [0]


def ring_pairs(n):
    order = ring_order(n)
    return [(order[i], order[(i + 1) % n]) for i in range(n)]


def hop(x):
    return lax.ppermute(x, "z", ring_pairs(lax.axis_size("z")))


def ring_sources(n):
    order = ring_order(n)
    spot = {place: at for at, place in enumerate(order)}
    return [[order[(spot[z] - k) % n] for k in range(n)] for z in range(n)]


def pick(options, which):
    out = options[0]
    for i in range(1, len(options)):
        out = jnp.where(which == i, options[i], out)
    return out


def both_cores(x):
    return jnp.stack([x, swap(x, "c")])


def core_order(mine, other, at):
    first = lax.axis_index("c") == 0
    return jnp.stack([jnp.where(first, mine, other), jnp.where(first, other, mine)], axis=at)


def ring_gather(x):
    n = lax.axis_size("z")
    parts = [x]
    for _ in range(n - 1):
        parts.append(hop(parts[-1]))
    return [both_cores(part) for part in parts]


def ring_scatter(partials):
    n = len(partials)

    def reduced(k):
        return partials[k][0] + swap(partials[k][1].astype(bf16), "c").astype(f32)

    total = reduced(1 % n)
    for s in range(n - 1):
        total = hop(total.astype(bf16)).astype(f32) + reduced((s + 2) % n)
    return total


def gather_plane(x):
    return lax.all_gather(x, ("y", "x"), axis=0, tiled=False)


def scatter_axis(x, axis):
    n = lax.axis_size(axis)
    if n != 2:
        return lax.psum_scatter(x.astype(bf16), axis, scatter_dimension=0, tiled=False).astype(f32)
    me = lax.axis_index(axis)
    own = lax.dynamic_index_in_dim(x, me, 0, keepdims=False)
    sent = lax.dynamic_index_in_dim(x, 1 - me, 0, keepdims=False)
    return own + swap(sent.astype(bf16), axis).astype(f32)


def scatter_plane(x):
    ny, nx = lax.axis_size("y"), lax.axis_size("x")
    half = (x.shape[-1] // 2) // 128 * 128
    x = x.reshape((ny, nx) + x.shape[1:])
    left, right = x[..., :half], x[..., half:]
    left = scatter_axis(scatter_axis(left, "y"), "x")
    right = scatter_axis(scatter_axis(jnp.swapaxes(right, 0, 1), "x"), "y")
    return jnp.concatenate([left, right], axis=-1)


def exchange(x):
    me = lax.axis_index("c")
    own = lax.dynamic_index_in_dim(x, me, 0, keepdims=False)
    other = swap(lax.dynamic_index_in_dim(x, 1 - me, 0, keepdims=False), "c")
    both = core_order(own, other, 1)
    return jnp.swapaxes(lax.all_to_all(both, "z", 0, 0, tiled=True), 0, 1)


def butterfly(x):
    for axis in ALL:
        n = lax.axis_size(axis)
        step = 1
        while step < n:
            x = x + lax.ppermute(x, axis, [(i, i ^ step) for i in range(n)])
            step *= 2
    return x


def doc_number(positions, doc_ends):
    counted = jnp.sum((positions[:, None] >= doc_ends[None, :]).astype(jnp.int32), axis=1)
    return jnp.where(positions < 0, -1, counted)


def windows(x, fill):
    pad = jnp.full((WINDOW,) + x.shape[1:], fill, x.dtype)
    shaped = jnp.concatenate([pad, x], axis=0).reshape((-1, WINDOW) + x.shape[1:])
    return jnp.concatenate([shaped[:-1], shaped[1:]], axis=1)


def unwindows(x):
    blocks = x.shape[0]
    zero = jnp.zeros((1, WINDOW) + x.shape[2:], x.dtype)
    below = jnp.concatenate([x[1:, :WINDOW], zero], axis=0)
    return (x[:, WINDOW:] + below).reshape((blocks * WINDOW,) + x.shape[2:])


def allowed_pairs(lengths, length):
    doc_ends = jnp.cumsum(lengths)
    docs = doc_number(jnp.arange(length, dtype=jnp.int32), doc_ends)
    offset_query = jnp.arange(WINDOW)[:, None]
    offset_key = jnp.arange(2 * WINDOW)[None, :]
    band = (offset_key > offset_query) & (offset_key <= offset_query + WINDOW)
    same = docs.reshape(-1, WINDOW)[:, :, None] == windows(docs, -1)[:, None, :]
    return (band[None] & same)[:, None]


def attention(query, key, value, lengths):
    length = query.shape[0]
    scale = 1.0 / math.sqrt(HEAD)
    allowed = allowed_pairs(lengths, length)
    query_blocks = query.reshape(-1, WINDOW, *query.shape[1:])
    key_window, value_window = windows(key, 0), windows(value, 0)
    raw = jnp.einsum("bqhd,bkhd->bhqk", query_blocks, key_window, preferred_element_type=f32)
    limited = jnp.where(allowed, raw * scale, masked_score)
    top = jnp.max(limited, axis=-1, keepdims=True)
    exped = jnp.exp(limited - top)
    probs = exped / jnp.sum(exped, axis=-1, keepdims=True)
    probs_b = probs.astype(bf16)
    mixed = jnp.einsum("bhqk,bkhd->bqhd", probs_b, value_window, preferred_element_type=f32)
    return mixed.reshape(query.shape).astype(bf16), probs


def attention_back(query, key, value, probs, grad):
    scale = 1.0 / math.sqrt(HEAD)
    probs_b = probs.astype(bf16)
    query_blocks = query.reshape(-1, WINDOW, *query.shape[1:])
    grad_blocks = grad.reshape(-1, WINDOW, *query.shape[1:])
    key_window, value_window = windows(key, 0), windows(value, 0)
    grad_probs = jnp.einsum(
        "bqhd,bkhd->bhqk", grad_blocks, value_window, preferred_element_type=f32
    )
    inner = jnp.sum(probs * grad_probs, axis=-1, keepdims=True)
    grad_scores = (probs * (grad_probs - inner)).astype(bf16)
    grad_query = (
        jnp.einsum("bhqk,bkhd->bqhd", grad_scores, key_window, preferred_element_type=f32) * scale
    )
    grad_key = (
        jnp.einsum("bhqk,bqhd->bkhd", grad_scores, query_blocks, preferred_element_type=f32) * scale
    )
    grad_value = jnp.einsum("bhqk,bqhd->bkhd", probs_b, grad_blocks, preferred_element_type=f32)
    return (
        grad_query.reshape(query.shape).astype(bf16),
        unwindows(grad_key).astype(bf16),
        unwindows(grad_value).astype(bf16),
    )


def rms_parts(values):
    inverse = lax.rsqrt(jnp.mean(values * values, axis=1, keepdims=True) + norm_eps)
    return (values * inverse, inverse)


def norm_back(grad_normed, gain, normed, inverse):
    scaled = grad_normed * gain
    back = inverse * (scaled - normed * jnp.mean(scaled * normed, axis=1, keepdims=True))
    return (back, jnp.sum(grad_normed * normed, axis=0))


def body(
    tokens,
    cotangent,
    lengths,
    norm_attn,
    w_query,
    w_key,
    w_value,
    w_out,
    norm_ffn,
    w_gate,
    w_up,
    w_down,
):
    t, width = tokens.shape
    own_rows, hidden_width = w_gate.shape
    nz = lax.axis_size("z")
    plane = lax.axis_size("y") * lax.axis_size("x")
    z = lax.axis_index("z")
    sources = jnp.asarray(ring_sources(nz), jnp.int32)[z]
    feats = width // (2 * nz)
    heads_here = feats // HEAD
    block = hidden_width // (plane * 2 * nz)
    units = plane * block

    qkv = jnp.stack([w_query, w_key, w_value]).reshape(3, own_rows, 2, nz, feats)
    qkv = exchange(qkv.transpose(2, 3, 0, 1, 4))
    qkv = gather_plane(qkv.transpose(2, 0, 1, 3, 4))
    w_qkv = [qkv[:, i].reshape(width, feats) for i in range(3)]

    inputs = tokens.astype(f32)
    normed_attn, inverse_attn = rms_parts(inputs)
    normed_attn_b = (normed_attn * norm_attn).astype(bf16)
    attn_in = [part.reshape(2 * t, width) for part in ring_gather(normed_attn_b)]

    lengths_both = both_cores(lengths[0])
    w_out_all = lax.all_gather(w_out, ALL, axis=0, tiled=True)
    gate_up = jnp.stack([w_gate, w_up]).reshape(2, own_rows, plane, 2, nz, block)
    gate_up = exchange(
        gate_up.transpose(3, 4, 0, 1, 2, 5).reshape(2, nz, 2, own_rows, units)
    )
    gate_up = gather_plane(gate_up.transpose(2, 0, 1, 3, 4))
    w_gate_here, w_up_here = (gate_up[:, i].reshape(width, units) for i in range(2))
    w_down_here = gather_plane(w_down).reshape(units, width)
    cot = [part.reshape(2 * t, width) for part in ring_gather(cotangent)]

    projected = []
    for i in range(3):
        placed = jnp.zeros((nz, 2, t, feats), bf16)
        for k in range(nz):
            piece = dot(attn_in[k], w_qkv[i]).astype(bf16).reshape(1, 2, t, feats)
            placed = lax.dynamic_update_slice(placed, piece, (sources[k], 0, 0, 0))
        projected.append(
            placed.transpose(1, 0, 2, 3).reshape(2, nz * t, heads_here, HEAD)
        )
    query, key, value = projected
    attended, probs = zip(
        *[attention(query[r], key[r], value[r], lengths_both[r]) for r in range(2)], strict=True
    )
    mine = attended[0].reshape(nz, t, feats)
    other = swap(attended[1].reshape(nz, t, feats), "c")
    mixed = lax.all_to_all(core_order(mine, other, 2), "z", 0, 0, tiled=True)
    attended_b = mixed.transpose(1, 2, 0, 3).reshape(t, width)

    middle = inputs + dot(attended_b, w_out_all)
    normed_ffn, inverse_ffn = rms_parts(middle)
    normed_ffn_b = (normed_ffn * norm_ffn).astype(bf16)

    ffn_in = [part.reshape(2 * t, width) for part in ring_gather(normed_ffn_b)]
    hidden, grad_gate, grad_up, out_parts, grad_parts = [], [], [], [], []
    for k in range(nz):
        gate = dot(ffn_in[k], w_gate_here)
        up = dot(ffn_in[k], w_up_here)
        sig = jax.nn.sigmoid(gate)
        silu = gate * sig
        hidden_k = (silu * up).astype(bf16)
        grad_hidden = dot_nt(cot[k], w_down_here)
        grad_gate_k = (grad_hidden * up * sig * (1.0 + gate * (1.0 - sig))).astype(bf16)
        grad_up_k = (grad_hidden * silu).astype(bf16)
        hidden.append(hidden_k)
        grad_gate.append(grad_gate_k)
        grad_up.append(grad_up_k)
        out_parts.append(dot(hidden_k, w_down_here).reshape(2, t, width))
        grad_parts.append(
            (dot_nt(grad_gate_k, w_gate_here) + dot_nt(grad_up_k, w_up_here)).reshape(2, t, width)
        )
    grad_normed_ffn = ring_scatter(grad_parts)
    back_ffn, gain_ffn_part = norm_back(grad_normed_ffn, norm_ffn, normed_ffn, inverse_ffn)
    grad_middle = cotangent.astype(f32) + back_ffn
    grad_branch_b = grad_middle.astype(bf16)

    grad_att = dot_nt(grad_branch_b, w_out_all).astype(bf16).reshape(t, 2, nz, feats)
    grad_att = lax.all_to_all(grad_att.transpose(2, 1, 0, 3), "z", 0, 0, tiled=True)
    me = lax.axis_index("c")
    grad_own = lax.dynamic_index_in_dim(grad_att, me, 1, keepdims=False)
    grad_other = swap(lax.dynamic_index_in_dim(grad_att, 1 - me, 1, keepdims=False), "c")
    grad_rows = [
        part.reshape(nz * t, heads_here, HEAD) for part in (grad_own, grad_other)
    ]
    grads = [
        attention_back(query[r], key[r], value[r], probs[r], grad_rows[r]) for r in range(2)
    ]
    grad_qkv = [
        jnp.stack([grads[r][i].reshape(nz, t, feats) for r in range(2)], axis=1)
        for i in range(3)
    ]
    grad_qkv = [
        [
            lax.dynamic_index_in_dim(part, sources[k], 0, keepdims=False).reshape(2 * t, feats)
            for k in range(nz)
        ]
        for part in grad_qkv
    ]
    grad_normed_attn = ring_scatter(
        [
            sum(dot_nt(grad_qkv[i][k], w_qkv[i]) for i in range(3)).reshape(2, t, width)
            for k in range(nz)
        ]
    )
    back_attn, gain_attn_part = norm_back(grad_normed_attn, norm_attn, normed_attn, inverse_attn)
    token_grad = grad_middle + back_attn
    gains = butterfly(jnp.stack([gain_attn_part, gain_ffn_part]))

    activations = (middle + ring_scatter(out_parts)).astype(bf16)

    cot_all = jnp.concatenate(cot)
    ffn_all = jnp.concatenate(ffn_in)
    attn_all = jnp.concatenate(attn_in)
    grad_w_down = scatter_plane(dot_tn(jnp.concatenate(hidden), cot_all).reshape(plane, block, width))

    grad_w_out = dot_tn(attended_b, grad_branch_b).reshape(plane, 2, nz * own_rows, width)
    grad_w_out = grad_w_out.transpose(1, 0, 2, 3)
    grad_w_out = scatter_plane(scatter_axis(grad_w_out, "c")).reshape(nz, own_rows, width)
    total = lax.dynamic_index_in_dim(grad_w_out, sources[1 % nz], 0, keepdims=False)
    for s in range(nz - 1):
        total = hop(total.astype(bf16)).astype(f32) + lax.dynamic_index_in_dim(
            grad_w_out, sources[(s + 2) % nz], 0, keepdims=False
        )
    grad_w_out = total

    def columns_home(parts, wide):
        parts = jnp.stack(
            [part.reshape(plane, 2, nz, own_rows, wide) for part in parts], axis=3
        )
        parts = scatter_plane(parts).astype(bf16)
        return exchange(parts)

    grad_gu = columns_home(
        [dot_tn(ffn_all, jnp.concatenate(grad_gate)), dot_tn(ffn_all, jnp.concatenate(grad_up))],
        units,
    ).reshape(2, nz, 2, own_rows, plane, block)
    grad_gu = grad_gu.transpose(2, 3, 4, 0, 1, 5).reshape(2, own_rows, hidden_width).astype(f32)
    grad_three = columns_home(
        [dot_tn(attn_all, jnp.concatenate(grad_qkv[i])) for i in range(3)], feats
    )
    grad_three = grad_three.transpose(2, 3, 0, 1, 4).reshape(3, own_rows, width).astype(f32)
    return (
        activations,
        token_grad,
        gains[0],
        grad_three[0],
        grad_three[1],
        grad_three[2],
        grad_w_out,
        gains[1],
        grad_gu[0],
        grad_gu[1],
        grad_w_down,
    )


def solution(mesh):
    dp, seq = mesh.shape["dp"], mesh.shape["seq"]
    grid = Mesh(mesh.devices.reshape(dp // 4, 2, 2, seq), ALL)
    split = P(ALL, None)
    return jax.shard_map(
        body,
        mesh=grid,
        in_specs=(split, split, P(("y", "x", "c"), None), P())
        + (split,) * 4
        + (P(),)
        + (split,) * 3,
        out_specs=(split, split, P(), split, split, split, split, P(), split, split, split),
        check_vma=False,
    )
```

```python
import functools
import math

import jax
import jax.numpy as jnp
from jax import lax
from jax.experimental import pallas as pl
from jax.experimental.pallas import tpu as pltpu
from jax.sharding import Mesh
from jax.sharding import PartitionSpec as P

HEADS = 16
HEAD = 128
WINDOW = 64
BLOCK = 128

ALL = ("p", "c", "z")
norm_eps = 1e-05
masked_score = -1e30
f32 = jnp.float32
bf16 = jnp.bfloat16


def dot(left, right, dims=((1,), (0,))):
    return lax.dot_general(left, right, (dims, ((), ())), preferred_element_type=f32)


def dot_nt(left, right):
    return dot(left, right, ((1,), (1,)))


def dot_tn(left, right):
    return dot(left, right, ((0,), (0,)))


def cross(x, axis, by):
    n = lax.axis_size(axis)
    return lax.ppermute(x, axis, [(i, i ^ by) for i in range(n)])


def ring_order(n):
    return list(range(1, n, 2)) + list(range(n - 2, -1, -2)) if n > 1 else [0]


def hop(x):
    n = lax.axis_size("z")
    order = ring_order(n)
    return lax.ppermute(x, "z", [(order[i], order[(i + 1) % n]) for i in range(n)])


def ring_sources(n):
    order = ring_order(n)
    spot = {place: at for at, place in enumerate(order)}
    return [[order[(spot[z] - k) % n] for k in range(n)] for z in range(n)]


def placed(parts, sources):
    out = jnp.zeros((len(parts),) + parts[0].shape, parts[0].dtype)
    for k, part in enumerate(parts):
        out = lax.dynamic_update_slice(out, part[None], (sources[k],) + (0,) * part.ndim)
    return out.reshape((-1,) + parts[0].shape[1:])


def gather_rows(x):
    return lax.all_gather(x, ("c", "p"), axis=0, tiled=False)


def indexed(x, at, axis):
    return lax.dynamic_index_in_dim(x, at, axis, keepdims=False)


def after(x, *others):
    return lax.optimization_barrier((x, others))[0]


def blocks_in_order(x, order):
    wide = x.shape[1] // len(order)
    return jnp.concatenate([x[:, i * wide : (i + 1) * wide] for i in order], axis=1)


def regrouped(x, n):
    return blocks_in_order(x, [2 * i + c for c in range(2) for i in range(n)])


def ungrouped(x, n):
    return blocks_in_order(x, [c * n + i for i in range(n) for c in range(2)])


def tick(jobs, also=()):
    operands = lax.optimization_barrier([operand for _, operand in jobs])
    results = [job(operand) for (job, _), operand in zip(jobs, operands, strict=True)]
    return lax.optimization_barrier((results, also))


def crossing(axis, by):
    return lambda x: cross(x, axis, by)


def exchange(x):
    return lax.all_to_all(x, "z", 0, 0, tiled=True)


def half_rows(left, right, at):
    half = left.shape[1] // 2
    return dot_tn(lax.dynamic_slice_in_dim(left, at * half, half, 1), right)


def plus(kept, came):
    return kept.astype(f32) + came.astype(f32)


def plane_open(x):
    n, me = lax.axis_size("p"), lax.axis_index("p")
    if n != 4:
        x = x.reshape((n, -1) + x.shape[1:])
        sent = [indexed(x, me ^ by, 0) for by in range(1, n)]
        return [(crossing("p", by), sent[by - 1]) for by in range(1, n)], indexed(x, me, 0)
    half = x.shape[1] // 256 * 128
    x = x.reshape((2, 2, -1) + x.shape[1:])
    left, right = x[..., :half], x[..., half:]
    high, low = me // 2, me % 2
    return [
        (crossing("p", 2), indexed(left, 1 - high, 0)),
        (crossing("p", 1), indexed(right, 1 - low, 1)),
    ], (indexed(left, high, 0), indexed(right, low, 1))


def plane_turn(came, kept):
    n, me = lax.axis_size("p"), lax.axis_index("p")
    if n != 4:
        return [], sum(part.astype(f32) for part in [kept, *came])
    high, low = me // 2, me % 2
    left, right = (plus(keep, part).astype(bf16) for keep, part in zip(kept, came, strict=True))
    return [
        (crossing("p", 1), indexed(left, 1 - low, 0)),
        (crossing("p", 2), indexed(right, 1 - high, 0)),
    ], (indexed(left, low, 0), indexed(right, high, 0))


def plane_close(came, kept):
    if not came:
        return kept
    return jnp.concatenate([plus(keep, part) for keep, part in zip(kept, came, strict=True)], axis=-1)


def butterfly(x):
    for axis in ALL:
        step = 1
        while step < lax.axis_size(axis):
            x = x + cross(x, axis, step)
            step *= 2
    return x


def doc_number(positions, doc_ends):
    return jnp.sum((positions[:, None] >= doc_ends[None, :]).astype(jnp.int32), axis=1)


def allowed_pairs(at, low, count, docs_down_ref, docs_across_ref):
    query_at = at + lax.broadcasted_iota(jnp.int32, (BLOCK, count), 0)
    key_at = low + lax.broadcasted_iota(jnp.int32, (BLOCK, count), 1)
    same = docs_down_ref[at : at + BLOCK, :] == docs_across_ref[:, low : low + count]
    return (key_at <= query_at) & (key_at > query_at - WINDOW) & same


def softmax(query, key, allowed):
    scores = jnp.where(allowed, dot_nt(query, key) * (1.0 / math.sqrt(HEAD)), masked_score)
    exped = jnp.exp(scores - jnp.max(scores, axis=-1, keepdims=True))
    return exped / jnp.sum(exped, axis=-1, keepdims=True)


def attention_kernel(qkv_ref, docs_down_ref, docs_across_ref, out_ref):
    length, width = out_ref.shape
    for at in range(0, length, BLOCK):
        low = max(0, at - BLOCK)
        allowed = allowed_pairs(at, low, at + BLOCK - low, docs_down_ref, docs_across_ref)
        for h in range(0, width, HEAD):
            query = qkv_ref[at : at + BLOCK, h : h + HEAD]
            key = qkv_ref[low : at + BLOCK, width + h : width + h + HEAD]
            value = qkv_ref[low : at + BLOCK, 2 * width + h : 2 * width + h + HEAD]
            probs = softmax(query, key, allowed)
            out_ref[at : at + BLOCK, h : h + HEAD] = dot(probs.astype(bf16), value).astype(bf16)


def attention_back_kernel(qkv_ref, grad_ref, docs_down_ref, docs_across_ref, out_ref):
    length, width = grad_ref.shape
    scale = 1.0 / math.sqrt(HEAD)
    pending = {}
    for at in range(0, length, BLOCK):
        low = max(0, at - BLOCK)
        allowed = allowed_pairs(at, low, at + BLOCK - low, docs_down_ref, docs_across_ref)
        for h in range(0, width, HEAD):
            query = qkv_ref[at : at + BLOCK, h : h + HEAD]
            key = qkv_ref[low : at + BLOCK, width + h : width + h + HEAD]
            value = qkv_ref[low : at + BLOCK, 2 * width + h : 2 * width + h + HEAD]
            grad = grad_ref[at : at + BLOCK, h : h + HEAD]
            probs = softmax(query, key, allowed)
            grad_probs = dot_nt(grad, value)
            inner = jnp.sum(probs * grad_probs, axis=-1, keepdims=True)
            grad_scores = (probs * (grad_probs - inner)).astype(bf16)
            out_ref[at : at + BLOCK, h : h + HEAD] = (dot(grad_scores, key) * scale).astype(bf16)
            grad_key = dot_tn(grad_scores, query) * scale
            grad_value = dot_tn(probs.astype(bf16), grad)
            if at > 0:
                before_key, before_value = pending[h]
                out_ref[low:at, width + h : width + h + HEAD] = (
                    before_key + grad_key[:BLOCK]
                ).astype(bf16)
                out_ref[low:at, 2 * width + h : 2 * width + h + HEAD] = (
                    before_value + grad_value[:BLOCK]
                ).astype(bf16)
            pending[h] = (grad_key[at - low :], grad_value[at - low :])
    for h, (last_key, last_value) in pending.items():
        out_ref[length - BLOCK :, width + h : width + h + HEAD] = last_key.astype(bf16)
        out_ref[length - BLOCK :, 2 * width + h : 2 * width + h + HEAD] = last_value.astype(bf16)


def local_kernel(kernel, columns, flops, *args):
    length = args[0].shape[0]
    return pl.pallas_call(
        kernel,
        out_shape=jax.ShapeDtypeStruct((length, columns), bf16),
        in_specs=[pl.BlockSpec(memory_space=pltpu.VMEM)] * len(args),
        out_specs=pl.BlockSpec(memory_space=pltpu.VMEM),
        compiler_params=pltpu.CompilerParams(vmem_limit_bytes=40 * 1024 * 1024),
        cost_estimate=pl.CostEstimate(flops=flops, bytes_accessed=length * columns * 8, transcendentals=0),
    )(*args)


def block_map(n, nz):
    return [(j % nz, (j // nz % 2) * n + j // nz // 2) for j in range(2 * n * nz)]


def spread_kernel(places, x_ref, out_ref):
    wide = x_ref.shape[1] // len(places)
    for j, (z, k) in enumerate(places):
        out_ref[z, :, k * wide : (k + 1) * wide] = x_ref[:, j * wide : (j + 1) * wide]


def collect_kernel(places, x_ref, out_ref):
    wide = out_ref.shape[1] // len(places)
    for j, (z, k) in enumerate(places):
        out_ref[:, j * wide : (j + 1) * wide] = x_ref[z, :, k * wide : (k + 1) * wide].astype(f32)


def spread(x, n, nz):
    rows, wide = x.shape
    return pl.pallas_call(
        functools.partial(spread_kernel, block_map(n, nz)),
        out_shape=jax.ShapeDtypeStruct((nz, rows, wide // nz), x.dtype),
        name="spread_units",
    )(x)


def collect(x, n):
    nz, rows, wide = x.shape
    return pl.pallas_call(
        functools.partial(collect_kernel, block_map(n, nz)),
        out_shape=jax.ShapeDtypeStruct((rows, wide * nz), f32),
        name="collect_units",
    )(x)


def rms_parts(values):
    inverse = lax.rsqrt(jnp.mean(values * values, axis=1, keepdims=True) + norm_eps)
    return (values * inverse, inverse)


def norm_back(grad_normed, gain, normed, inverse):
    scaled = grad_normed * gain
    back = inverse * (scaled - normed * jnp.mean(scaled * normed, axis=1, keepdims=True))
    return (back, jnp.sum(grad_normed * normed, axis=0))


def body(
    tokens,
    cotangent,
    lengths,
    norm_attn,
    w_query,
    w_key,
    w_value,
    w_out,
    norm_ffn,
    w_gate,
    w_up,
    w_down,
):
    t, width = tokens.shape
    own_rows, hidden_width = w_gate.shape
    nz = lax.axis_size("z")
    groups = lax.axis_size("p") * 2
    sources = jnp.asarray(ring_sources(nz), jnp.int32)[lax.axis_index("z")]
    feats = width // nz
    block = hidden_width // (groups * nz)
    units = groups * block
    group_rows = nz * own_rows

    n = lax.axis_size("p")
    me, core = lax.axis_index("p"), lax.axis_index("c")
    hops = nz - 1

    inputs = tokens.astype(f32)
    normed_attn, inverse_attn = rms_parts(inputs)
    normed_attn_b = regrouped((normed_attn * norm_attn).astype(bf16), n)

    w_down_here = gather_rows(w_down).reshape(units, width)
    qkv = jnp.concatenate(
        [w.reshape(own_rows, nz, feats) for w in (w_query, w_key, w_value)], axis=2
    ).transpose(1, 0, 2)
    qkv = exchange(qkv)
    w_qkv = gather_rows(qkv).reshape(width, 3 * feats)

    attn_in, out_rows = [after(normed_attn_b, qkv)], [w_out]
    for k in range(hops):
        parts, w_down_here = tick([(hop, attn_in[-1]), (hop, out_rows[-1])], w_down_here)
        attn_in.append(parts[0])
        out_rows.append(parts[1])
    attn_in = placed(attn_in, sources)
    w_out_all = gather_rows(placed(out_rows, sources)).reshape(width, width)

    gate_up = jnp.concatenate([spread(w, n, nz) for w in (w_gate, w_up)], axis=2)
    gate_up = exchange(after(gate_up, attn_in))
    w_gate_up = gather_rows(gate_up).reshape(width, 2 * units)
    cot = [after(cotangent, gate_up)]

    docs = doc_number(jnp.arange(nz * t, dtype=jnp.int32), jnp.cumsum(lengths[0]))
    docs_down, docs_across = docs[:, None], docs[None, :]
    flops = 4 * nz * t * 2 * BLOCK * feats
    def cot_hop():
        return [(hop, cot[-1])] if len(cot) < nz else []

    three = dot(attn_in, w_qkv).astype(bf16)
    attended = local_kernel(attention_kernel, feats, flops, three, docs_down, docs_across)
    part, attended = tick(cot_hop(), attended)
    cot += part
    (attended,), _ = tick([(exchange, attended.reshape(nz, t, feats))])
    attended_b = regrouped(attended.transpose(1, 0, 2).reshape(t, width), n)
    middle = inputs + dot(attended_b, w_out_all)
    normed_ffn, inverse_ffn = rms_parts(middle)
    normed_ffn_b = regrouped((normed_ffn * norm_ffn).astype(bf16), n)
    part, normed_ffn_b = tick(cot_hop(), normed_ffn_b)
    cot += part

    ffn_in = [normed_ffn_b]
    for _ in range(hops):
        (part, *more), _ = tick([(hop, ffn_in[-1])] + cot_hop())
        ffn_in.append(part)
        cot += more

    def next_hop(total, partials, s, jobs=(), also=()):
        first = partials[1 % nz] if s == 0 else total
        (part, *rest), also = tick([(hop, first.astype(bf16)), *jobs], also)
        return part.astype(f32) + partials[(s + 2) % nz], rest, also

    def chunks(x):
        return [x[k * t : (k + 1) * t] for k in range(nz)]

    left, right = jnp.concatenate(ffn_in), jnp.concatenate(cot)
    both = dot(left, w_gate_up)
    gate, up = both[:, :units], both[:, units:]
    sig = jax.nn.sigmoid(gate)
    silu = gate * sig
    hidden = (silu * up).astype(bf16)
    grad_hidden = dot_nt(right, w_down_here)
    grad_gate_up = jnp.concatenate(
        [grad_hidden * up * sig * (1.0 + gate * (1.0 - sig)), grad_hidden * silu], axis=1
    ).astype(bf16)
    grad_parts = chunks(dot_nt(grad_gate_up, w_gate_up))

    gu_other = half_rows(left, grad_gate_up, 1 - core).astype(bf16)
    total, _, gu_other = next_hop(None, grad_parts, 0, (), gu_other)
    down = dot_tn(hidden, right).astype(bf16).reshape(2, n * block, width)
    down_own, down_other = indexed(down, core, 0), indexed(down, 1 - core, 0)
    total, (gu_other,), (down_own, down_other) = next_hop(
        total, grad_parts, 1, [(crossing("c", 1), gu_other)], (down_own, down_other)
    )
    gu = plus(half_rows(left, grad_gate_up, core), gu_other).astype(bf16)
    gate_jobs, gate_kept = plane_open(gu[:, :units])
    up_jobs, up_kept = plane_open(gu[:, units:])
    total, gate_came, up_jobs_sent = next_hop(
        total, grad_parts, 2, gate_jobs, [part for _, part in up_jobs]
    )
    up_jobs = [(job, part) for (job, _), part in zip(up_jobs, up_jobs_sent, strict=True)]
    for s in range(3, hops):
        total, _, _ = next_hop(total, grad_parts, s)
    gate_jobs, gate_kept = plane_turn(gate_came, gate_kept)
    grad_normed_ffn = ungrouped(total, n)
    back_ffn, gain_ffn_part = norm_back(grad_normed_ffn, norm_ffn, normed_ffn, inverse_ffn)
    grad_middle = cotangent.astype(f32) + back_ffn
    grad_branch_b = grad_middle.astype(bf16)
    grad_att = ungrouped(dot_nt(grad_branch_b, w_out_all).astype(bf16), n).reshape(t, nz, feats)
    grad_att = grad_att.transpose(1, 0, 2)
    out_other = half_rows(attended_b, grad_branch_b, 1 - core).astype(bf16)
    (grad_att, *up_came), out_other = tick([(exchange, grad_att), *up_jobs], out_other)
    up_jobs, up_kept = plane_turn(up_came, up_kept)
    out_parts = chunks(dot(hidden, w_down_here))
    grad_three = local_kernel(
        attention_back_kernel,
        3 * feats,
        3 * flops,
        three,
        grad_att.reshape(nz * t, feats),
        docs_down,
        docs_across,
    )
    attn_back = dot_nt(grad_three, w_qkv).reshape(nz, t, width)
    attn_back = [indexed(attn_back, sources[k], 0) for k in range(nz)]
    out_total, came, (grad_three, attn_back) = next_hop(
        None,
        out_parts,
        0,
        [(crossing("c", 1), out_other), (crossing("c", 1), down_other), *gate_jobs, *up_jobs],
        (grad_three, attn_back),
    )
    out_other, down_other, *came = came
    gate_came, up_came = came[: len(gate_jobs)], came[len(gate_jobs) :]
    grad_gate = plane_close(gate_came, gate_kept).astype(bf16).reshape(nz, own_rows, units)
    grad_up = plane_close(up_came, up_kept).astype(bf16).reshape(nz, own_rows, units)

    out_sum = plus(half_rows(attended_b, grad_branch_b, core), out_other).astype(bf16)
    down_sum = plus(down_own, down_other).astype(bf16)
    out_jobs, out_kept = plane_open(out_sum)
    qkv_other = half_rows(attn_in, grad_three, 1 - core).astype(bf16)
    total, _, qkv_other = next_hop(None, attn_back, 0, (), qkv_other)
    total, (qkv_other, *out_came), _ = next_hop(
        total, attn_back, 1, [(crossing("c", 1), qkv_other), *out_jobs]
    )
    qkv_sum = plus(half_rows(attn_in, grad_three, core), qkv_other).astype(bf16)
    out_jobs, out_kept = plane_turn(out_came, out_kept)
    total, out_came, (qkv_sum, down_sum) = next_hop(
        total, attn_back, 2, out_jobs, (qkv_sum, down_sum)
    )
    for s in range(3, hops):
        total, _, _ = next_hop(total, attn_back, s)
    grad_w_out = plane_close(out_came, out_kept).reshape(nz, own_rows, width)
    grad_w_out = [indexed(grad_w_out, sources[k], 0) for k in range(nz)]
    grad_normed_attn = ungrouped(total, n)
    back_attn, gain_attn_part = norm_back(grad_normed_attn, norm_attn, normed_attn, inverse_attn)
    token_grad = grad_middle + back_attn

    qkv_jobs, qkv_kept = plane_open(qkv_sum)
    down_jobs, down_kept = plane_open(down_sum)
    w_out_total, (grad_gate, *qkv_came), _ = next_hop(
        None, grad_w_out, 0, [(exchange, grad_gate), *qkv_jobs]
    )
    qkv_jobs, qkv_kept = plane_turn(qkv_came, qkv_kept)
    gains = butterfly(jnp.stack([gain_attn_part, gain_ffn_part]))
    w_out_total, (grad_up, *qkv_came), gains = next_hop(
        w_out_total, grad_w_out, 1, [(exchange, grad_up), *qkv_jobs], gains
    )
    grad_qkv = plane_close(qkv_came, qkv_kept).astype(bf16).reshape(nz, own_rows, 3 * feats)
    grad_w_gate = collect(grad_gate, n)
    w_out_total, (grad_qkv, *down_came), grad_w_gate = next_hop(
        w_out_total, grad_w_out, 2, [(exchange, grad_qkv), *down_jobs], grad_w_gate
    )
    down_jobs, down_kept = plane_turn(down_came, down_kept)
    grad_w_up = collect(grad_up, n)
    out_total, _, _ = next_hop(out_total, out_parts, 1, (), grad_w_up)
    out_total, down_came, _ = next_hop(out_total, out_parts, 2, down_jobs)
    for s in range(3, hops):
        w_out_total, _, _ = next_hop(w_out_total, grad_w_out, s)
        out_total, _, _ = next_hop(out_total, out_parts, s)
    grad_w_down = plane_close(down_came, down_kept)
    grad_w_out = w_out_total
    activations = (middle + out_total).astype(bf16)
    grad_w_query, grad_w_key, grad_w_value = (
        grad_qkv[:, :, i * feats : (i + 1) * feats]
        .transpose(1, 0, 2)
        .reshape(own_rows, width)
        .astype(f32)
        for i in range(3)
    )
    return (
        activations,
        token_grad,
        gains[0],
        grad_w_query,
        grad_w_key,
        grad_w_value,
        grad_w_out,
        gains[1],
        grad_w_gate,
        grad_w_up,
        grad_w_down,
    )


def solution(mesh):
    dp, seq = mesh.shape["dp"], mesh.shape["seq"]
    grid = Mesh(mesh.devices.reshape(dp // 2, 2, seq), ALL)
    split = P(ALL, None)
    return jax.shard_map(
        body,
        mesh=grid,
        in_specs=(split, split, P(("p", "c"), None), P())
        + (split,) * 4
        + (P(),)
        + (split,) * 3,
        out_specs=(split, split, P(), split, split, split, split, P(), split, split, split),
        check_vma=False,
    )
```

```python
import functools
import math

import jax
import jax.numpy as jnp
from jax import lax
from jax.experimental import pallas as pl
from jax.experimental.pallas import tpu as pltpu
from jax.sharding import Mesh
from jax.sharding import PartitionSpec as P

HEADS = 16
HEAD = 128
WINDOW = 64
BLOCK = 128
PARTS = 1

ALL = ("p", "c", "z")
norm_eps = 1e-05
masked_score = -1e30
f32 = jnp.float32
bf16 = jnp.bfloat16


def dot(left, right, dims=((1,), (0,))):
    return lax.dot_general(left, right, (dims, ((), ())), preferred_element_type=f32)


def dot_nt(left, right):
    return dot(left, right, ((1,), (1,)))


def dot_tn(left, right):
    return dot(left, right, ((0,), (0,)))


def cross(x, axis, by):
    n = lax.axis_size(axis)
    return lax.ppermute(x, axis, [(i, i ^ by) for i in range(n)])


def ring_order(n):
    return list(range(1, n, 2)) + list(range(n - 2, -1, -2)) if n > 1 else [0]


def hop(x):
    n = lax.axis_size("z")
    order = ring_order(n)
    return lax.ppermute(x, "z", [(order[i], order[(i + 1) % n]) for i in range(n)])


def ring_sources(n):
    order = ring_order(n)
    spot = {place: at for at, place in enumerate(order)}
    return [[order[(spot[z] - k) % n] for k in range(n)] for z in range(n)]


def placed(parts, sources):
    out = jnp.zeros((len(parts),) + parts[0].shape, parts[0].dtype)
    for k, part in enumerate(parts):
        out = lax.dynamic_update_slice(out, part[None], (sources[k],) + (0,) * part.ndim)
    return out.reshape((-1,) + parts[0].shape[1:])


def gather_rows(x):
    return lax.all_gather(x, ("c", "p"), axis=0, tiled=False)


def indexed(x, at, axis):
    return lax.dynamic_index_in_dim(x, at, axis, keepdims=False)


def after(x, *others):
    return lax.optimization_barrier((x, others))[0]


def blocks_in_order(x, order):
    wide = x.shape[1] // len(order)
    return jnp.concatenate([x[:, i * wide : (i + 1) * wide] for i in order], axis=1)


def regrouped(x, n):
    return blocks_in_order(x, [2 * i + c for c in range(2) for i in range(n)])


def ungrouped(x, n):
    return blocks_in_order(x, [c * n + i for i in range(n) for c in range(2)])


def tick(jobs, also=()):
    operands = lax.optimization_barrier([operand for _, operand in jobs])
    results = [job(operand) for (job, _), operand in zip(jobs, operands, strict=True)]
    return lax.optimization_barrier((results, also))


def crossing(axis, by):
    return lambda x: cross(x, axis, by)


def exchange(x):
    return lax.all_to_all(x, "z", 0, 0, tiled=True)


def plus(kept, came):
    return kept.astype(f32) + came.astype(f32)


class Line:
    def __init__(self):
        self.token = lax.optimization_barrier(jnp.zeros((8, 128), f32))

    def hold(self, *values):
        values, self.token = lax.optimization_barrier((values, self.token))
        return values[0] if len(values) == 1 else values

    def __call__(self, piece, *values):
        values, self.token = lax.optimization_barrier((values, self.token))
        return self.hold(piece(*values))


def plane_sent(parts, first, last):
    return [cross(parts[by - 1], "p", by) for by in range(first, last)]


def summed(*parts):
    return sum(part.astype(f32) for part in parts)


def spread_sums(x, axis):
    return [cross(x, axis, by) for by in range(1, lax.axis_size(axis))]


def paired_sum(parts):
    while len(parts) > 1:
        parts = [parts[i] + parts[i + 1] for i in range(0, len(parts), 2)]
    return parts[0]


def doc_number(positions, doc_ends):
    return jnp.sum((positions[:, None] >= doc_ends[None, :]).astype(jnp.int32), axis=1)


def allowed_pairs(at, low, count, docs_down_ref, docs_across_ref):
    query_at = at + lax.broadcasted_iota(jnp.int32, (BLOCK, count), 0)
    key_at = low + lax.broadcasted_iota(jnp.int32, (BLOCK, count), 1)
    same = docs_down_ref[at : at + BLOCK, :] == docs_across_ref[:, low : low + count]
    return (key_at <= query_at) & (key_at > query_at - WINDOW) & same


def softmax(query, key, allowed):
    scores = jnp.where(allowed, dot_nt(query, key) * (1.0 / math.sqrt(HEAD)), masked_score)
    exped = jnp.exp(scores - jnp.max(scores, axis=-1, keepdims=True))
    return exped / jnp.sum(exped, axis=-1, keepdims=True)


def attention_kernel(qkv_ref, docs_down_ref, docs_across_ref, out_ref):
    length, width = out_ref.shape
    for at in range(0, length, BLOCK):
        low = max(0, at - BLOCK)
        allowed = allowed_pairs(at, low, at + BLOCK - low, docs_down_ref, docs_across_ref)
        for h in range(0, width, HEAD):
            query = qkv_ref[at : at + BLOCK, h : h + HEAD]
            key = qkv_ref[low : at + BLOCK, width + h : width + h + HEAD]
            value = qkv_ref[low : at + BLOCK, 2 * width + h : 2 * width + h + HEAD]
            probs = softmax(query, key, allowed)
            out_ref[at : at + BLOCK, h : h + HEAD] = dot(probs.astype(bf16), value).astype(bf16)


def attention_back_kernel(qkv_ref, grad_ref, docs_down_ref, docs_across_ref, out_ref):
    length, width = grad_ref.shape
    scale = 1.0 / math.sqrt(HEAD)
    pending = {}
    for at in range(0, length, BLOCK):
        low = max(0, at - BLOCK)
        allowed = allowed_pairs(at, low, at + BLOCK - low, docs_down_ref, docs_across_ref)
        for h in range(0, width, HEAD):
            query = qkv_ref[at : at + BLOCK, h : h + HEAD]
            key = qkv_ref[low : at + BLOCK, width + h : width + h + HEAD]
            value = qkv_ref[low : at + BLOCK, 2 * width + h : 2 * width + h + HEAD]
            grad = grad_ref[at : at + BLOCK, h : h + HEAD]
            probs = softmax(query, key, allowed)
            grad_probs = dot_nt(grad, value)
            inner = jnp.sum(probs * grad_probs, axis=-1, keepdims=True)
            grad_scores = (probs * (grad_probs - inner)).astype(bf16)
            out_ref[at : at + BLOCK, h : h + HEAD] = (dot(grad_scores, key) * scale).astype(bf16)
            grad_key = dot_tn(grad_scores, query) * scale
            grad_value = dot_tn(probs.astype(bf16), grad)
            if at > 0:
                before_key, before_value = pending[h]
                out_ref[low:at, width + h : width + h + HEAD] = (
                    before_key + grad_key[:BLOCK]
                ).astype(bf16)
                out_ref[low:at, 2 * width + h : 2 * width + h + HEAD] = (
                    before_value + grad_value[:BLOCK]
                ).astype(bf16)
            pending[h] = (grad_key[at - low :], grad_value[at - low :])
    for h, (last_key, last_value) in pending.items():
        out_ref[length - BLOCK :, width + h : width + h + HEAD] = last_key.astype(bf16)
        out_ref[length - BLOCK :, 2 * width + h : 2 * width + h + HEAD] = last_value.astype(bf16)


def local_kernel(kernel, columns, *args):
    length = args[0].shape[0]
    return pl.pallas_call(
        kernel,
        out_shape=jax.ShapeDtypeStruct((length, columns), bf16),
        in_specs=[pl.BlockSpec(memory_space=pltpu.VMEM)] * len(args),
        out_specs=pl.BlockSpec(memory_space=pltpu.VMEM),
        compiler_params=kernel_params(10),
        cost_estimate=kernel_cost(5),
    )(*args)


def unit_pieces(n, nz, block, tile):
    pieces = []
    for j in range(2 * n * nz):
        start = ((j // nz % 2) * n + j // nz // 2) * block
        at = start
        while at < start + block:
            end = min(start + block, (at // tile + 1) * tile)
            column = at // tile * 2 * tile + at % tile
            pieces.append((j * block + at - start, j % nz, column, column + tile, end - at))
            at = end
    return pieces


def spread_kernel(pieces, gate_ref, up_ref, out_ref):
    for stored, z, gate_at, up_at, size in pieces:
        out_ref[z, :, gate_at : gate_at + size] = gate_ref[:, stored : stored + size]
        out_ref[z, :, up_at : up_at + size] = up_ref[:, stored : stored + size]


def collect_kernel(pieces, cut, first_ref, second_ref, gate_ref, up_ref):
    for stored, z, gate_at, up_at, size in pieces:
        for at, ref in ((gate_at, gate_ref), (up_at, up_ref)):
            inside = min(max(cut - at, 0), size)
            for source, low, start, count in (
                (first_ref, at, stored, inside),
                (second_ref, at + inside - cut, stored + inside, size - inside),
            ):
                if count:
                    ref[:, start : start + count] = source[z, :, low : low + count].astype(f32)


def spread(gate, up, nz, pieces):
    rows, wide = gate.shape
    return pl.pallas_call(
        functools.partial(spread_kernel, pieces),
        out_shape=jax.ShapeDtypeStruct((nz, rows, 2 * wide // nz), gate.dtype),
        name="spread_units",
    )(gate, up)


def collect(first, second, pieces):
    nz, rows, cut = first.shape
    wide = nz * (cut + second.shape[2]) // 2
    return pl.pallas_call(
        functools.partial(collect_kernel, pieces, cut),
        out_shape=[jax.ShapeDtypeStruct((rows, wide), f32)] * 2,
        name="collect_units",
    )(first, second)


def units_back(gate, up, grad_hidden):
    sig = jax.nn.sigmoid(gate)
    silu = gate * sig
    return (
        (silu * up).astype(bf16),
        (grad_hidden * up * sig * (1.0 + gate * (1.0 - sig))).astype(bf16),
        (grad_hidden * silu).astype(bf16),
    )


def feed_kernel(nz, places_ref, *refs):
    lefts, rights = refs[:nz], refs[nz : 2 * nz]
    gate_up_ref, down_ref, hidden_ref, grad_ref, left_ref, right_ref = refs[2 * nz :]
    t, tile = lefts[0].shape[0], down_ref.shape[0]

    @pl.when(pl.program_id(0) == 0)
    def _():
        for k in range(nz):
            start = pl.multiple_of(places_ref[k] * t, t)
            left_ref[pl.ds(start, t), :] = lefts[k][...]
            right_ref[pl.ds(start, t), :] = rights[k][...]

    both = dot(left_ref[...], gate_up_ref[...])
    grad_hidden = dot_nt(right_ref[...], down_ref[...])
    hidden, grad_gate, grad_up = units_back(both[:, :tile], both[:, tile:], grad_hidden)
    hidden_ref[...] = hidden
    grad_ref[:, :tile] = grad_gate
    grad_ref[:, tile:] = grad_up


def feed(lefts, rights, places, w_gate_up, w_down, tile):
    nz, (t, width) = len(lefts), lefts[0].shape
    units = w_down.shape[0]
    if tile != 128:
        left, right = placed(lefts, places), placed(rights, places)
        both = dot(left, w_gate_up)
        grad_hidden = dot_nt(right, w_down)
        hidden, grad_gate, grad_up = units_back(both[:, :units], both[:, units:], grad_hidden)
        return hidden, jnp.concatenate([grad_gate, grad_up], axis=1), left, right
    rows = nz * t
    whole = pl.BlockSpec((t, width), lambda i, at: (0, 0))
    every = pl.BlockSpec((rows, width), lambda i, at: (0, 0))
    return pl.pallas_call(
        functools.partial(feed_kernel, nz),
        grid_spec=pltpu.PrefetchScalarGridSpec(
            num_scalar_prefetch=1,
            grid=(units // tile,),
            in_specs=[whole] * (2 * nz)
            + [
                pl.BlockSpec((width, 2 * tile), lambda i, at: (0, i)),
                pl.BlockSpec((tile, width), lambda i, at: (i, 0)),
            ],
            out_specs=[
                pl.BlockSpec((rows, tile), lambda i, at: (0, i)),
                pl.BlockSpec((rows, 2 * tile), lambda i, at: (0, i)),
                every,
                every,
            ],
        ),
        out_shape=[
            jax.ShapeDtypeStruct((rows, units), bf16),
            jax.ShapeDtypeStruct((rows, 2 * units), bf16),
            jax.ShapeDtypeStruct((rows, width), bf16),
            jax.ShapeDtypeStruct((rows, width), bf16),
        ],
        compiler_params=kernel_params(60),
        cost_estimate=kernel_cost(18),
        name="feed_units",
    )(places, *lefts, *rights, w_gate_up, w_down)


def kernel_cost(us):
    return pl.CostEstimate(flops=int(us * 1.15e9 * 0.5), bytes_accessed=0, transcendentals=0)


def kernel_params(mib):
    return pltpu.CompilerParams(vmem_limit_bytes=mib * 1024 * 1024)


def tile_of(columns, most=1408):
    return max(tile for tile in range(128, most + 1, 128) if columns % tile == 0)


def rows_kernel(n, mode, at_ref, left_ref, right_ref, *refs):
    flip_ref, total_ref = refs[-2:]
    came, outs = (refs[:0], refs[:-2]) if mode == "other" else (refs[:PARTS], refs[PARTS:-2])

    @pl.when(pl.program_id(0) == 0)
    def _():
        flip_ref[...] = left_ref[...].T

    total = dot(flip_ref[...], right_ref[...])
    size = total.shape[0] // PARTS
    for k in range(PARTS):
        part = total[k * size : (k + 1) * size]
        if mode == "other":
            outs[k][...] = part.astype(bf16)
        else:
            part = (part + came[k][...].astype(f32)).astype(bf16)
            into = outs[0] if mode == "whole" else total_ref
            into[k * size : (k + 1) * size, :] = part
    if mode == "cut":
        rest = total.shape[0] // n
        for by in range(n):
            start = pl.multiple_of((at_ref[1] ^ by) * rest, rest)
            outs[by][...] = total_ref[pl.ds(start, rest), :]


def rows_product(left, right, half, me, n, mode, came=(), first=0, last=None):
    t, rows = left.shape[0], left.shape[1] // 2
    last = right.shape[1] if last is None else last
    tile = tile_of(math.gcd(last - first, first) if first else last)
    rest, columns, off = rows // n, last - first, first // tile
    at = jnp.stack([half, me]).astype(jnp.int32)
    outs, height = {"whole": (1, rows), "cut": (n, rest), "other": (PARTS, rows // PARTS)}[mode]
    return pl.pallas_call(
        functools.partial(rows_kernel, n, mode),
        grid_spec=pltpu.PrefetchScalarGridSpec(
            num_scalar_prefetch=1,
            grid=(columns // tile,),
            in_specs=[
                pl.BlockSpec((t, rows), lambda i, at: (0, at[0])),
                pl.BlockSpec((t, tile), lambda i, at: (0, i + off)),
            ]
            + [pl.BlockSpec((rows // PARTS, tile), lambda i, at: (0, i + off))] * len(came),
            out_specs=[pl.BlockSpec((height, tile), lambda i, at: (0, i))] * outs,
            scratch_shapes=[pltpu.VMEM((rows, t), bf16), pltpu.VMEM((rows, tile), bf16)],
        ),
        out_shape=[jax.ShapeDtypeStruct((height, columns), bf16)] * outs,
        compiler_params=kernel_params(60),
        cost_estimate=kernel_cost(6.5),
        name="rows_product",
    )(at, left, right, *came)


def down_kernel(n, at_ref, left_ref, right_ref, *refs):
    outs, flip_ref, total_ref = refs[:-2], refs[-2], refs[-1]
    rest = outs[0].shape[0]

    @pl.when(pl.program_id(0) == 0)
    def _():
        flip_ref[...] = left_ref[...].T

    total_ref[...] = dot(flip_ref[...], right_ref[...]).astype(bf16)
    for k, out_ref in enumerate(outs):
        half = at_ref[0] if k < n else 1 - at_ref[0]
        start = (half * n + (at_ref[1] ^ (k % n))) * rest
        out_ref[...] = total_ref[pl.ds(pl.multiple_of(start, math.gcd(rest, 16)), rest), :]


def down_product(left, right, core, me, n):
    t, rows = left.shape
    columns = right.shape[1]
    tile = tile_of(columns)
    rest = rows // (2 * n)
    if rest % 16:
        full = dot_tn(left, right).astype(bf16).reshape(2, n, rest, columns)
        parts = [indexed(indexed(full, at, 0), me ^ by, 0) for at in (core, 1 - core) for by in range(n)]
        return parts[:n], parts[n:]
    parts = pl.pallas_call(
        functools.partial(down_kernel, n),
        grid_spec=pltpu.PrefetchScalarGridSpec(
            num_scalar_prefetch=1,
            grid=(columns // tile,),
            in_specs=[
                pl.BlockSpec((t, rows), lambda i, at: (0, 0)),
                pl.BlockSpec((t, tile), lambda i, at: (0, i)),
            ],
            out_specs=[pl.BlockSpec((rest, tile), lambda i, at: (0, i))] * (2 * n),
            scratch_shapes=[pltpu.VMEM((rows, t), bf16), pltpu.VMEM((rows, tile), bf16)],
        ),
        out_shape=[jax.ShapeDtypeStruct((rest, columns), bf16)] * (2 * n),
        compiler_params=kernel_params(60),
        cost_estimate=kernel_cost(7),
        name="down_product",
    )(jnp.stack([core, me]).astype(jnp.int32), left, right)
    return parts[:n], parts[n:]


def chunks_kernel(transposed, at_ref, x_ref, w_ref, *refs):
    outs, total_ref = refs[:-1], refs[-1]
    t = outs[0].shape[0]
    total_ref[...] = (dot_nt if transposed else dot)(x_ref[...], w_ref[...])
    for k, out_ref in enumerate(outs):
        start = pl.multiple_of(at_ref[k] * t, t)
        out_ref[...] = total_ref[pl.ds(start, t), :].astype(out_ref.dtype)


def chunks_product(x, w, places, transposed):
    rows, depth = x.shape
    n, columns = places.shape[0], w.shape[0 if transposed else 1]
    tile = tile_of(columns)
    w_spec = (
        pl.BlockSpec((tile, depth), lambda i, at: (i, 0))
        if transposed
        else pl.BlockSpec((depth, tile), lambda i, at: (0, i))
    )
    return pl.pallas_call(
        functools.partial(chunks_kernel, transposed),
        grid_spec=pltpu.PrefetchScalarGridSpec(
            num_scalar_prefetch=1,
            grid=(columns // tile,),
            in_specs=[pl.BlockSpec((rows, depth), lambda i, at: (0, 0)), w_spec],
            out_specs=[pl.BlockSpec((rows // n, tile), lambda i, at: (0, i))] * n,
            scratch_shapes=[pltpu.VMEM((rows, tile), f32)],
        ),
        out_shape=[
            jax.ShapeDtypeStruct((rows // n, columns), bf16 if k == 1 % n else f32) for k in range(n)
        ],
        compiler_params=kernel_params(60),
        cost_estimate=kernel_cost(8),
        name="chunks_product",
    )(places, x, w)


def heads_kernel(x_ref, w_ref, out_ref):
    out_ref[0] = dot_nt(x_ref[...], w_ref[...]).astype(bf16)


def heads_product(x, w, n, nz):
    rows, depth = x.shape
    rest, feats = w.shape[0] // (2 * n), w.shape[0] // nz
    per = feats // rest

    def place(i):
        block = i % n * 2 + i // n
        return (block // per, 0, block % per)

    return pl.pallas_call(
        heads_kernel,
        grid=(2 * n,),
        in_specs=[
            pl.BlockSpec((rows, depth), lambda i: (0, 0)),
            pl.BlockSpec((rest, depth), lambda i: (i, 0)),
        ],
        out_specs=pl.BlockSpec((1, rows, rest), place),
        out_shape=jax.ShapeDtypeStruct((nz, rows, feats), bf16),
        compiler_params=kernel_params(60),
        cost_estimate=kernel_cost(4),
        name="heads_product",
    )(x, w)


def rms_parts(values):
    inverse = lax.rsqrt(jnp.mean(values * values, axis=1, keepdims=True) + norm_eps)
    return (values * inverse, inverse)


def norm_back(grad_normed, gain, normed, inverse):
    scaled = grad_normed * gain
    back = inverse * (scaled - normed * jnp.mean(scaled * normed, axis=1, keepdims=True))
    return (back, jnp.sum(grad_normed * normed, axis=0))


def body(
    tokens,
    cotangent,
    lengths,
    norm_attn,
    w_query,
    w_key,
    w_value,
    w_out,
    norm_ffn,
    w_gate,
    w_up,
    w_down,
):
    t, width = tokens.shape
    own_rows, hidden_width = w_gate.shape
    nz = lax.axis_size("z")
    groups = lax.axis_size("p") * 2
    sources = jnp.asarray(ring_sources(nz), jnp.int32)[lax.axis_index("z")]
    feats = width // nz
    block = hidden_width // (groups * nz)
    units = groups * block
    group_rows = nz * own_rows

    n = lax.axis_size("p")
    me, core = lax.axis_index("p"), lax.axis_index("c")
    hops = nz - 1

    inputs = tokens.astype(f32)
    normed_attn, inverse_attn = rms_parts(inputs)
    normed_attn_b = regrouped((normed_attn * norm_attn).astype(bf16), n)

    w_down_here = gather_rows(w_down).reshape(units, width)
    qkv = jnp.concatenate(
        [w.reshape(own_rows, nz, feats) for w in (w_query, w_key, w_value)], axis=2
    ).transpose(1, 0, 2)
    qkv = exchange(qkv)
    w_qkv = gather_rows(qkv).reshape(width, 3 * feats)

    tile = 128 if units % 128 == 0 else units
    cut = -(-units // 256) * 256
    pieces = unit_pieces(n, nz, block, tile)
    gate_up = spread(w_gate, w_up, nz, pieces)
    attn_in, out_rows = [after(normed_attn_b, qkv)], [w_out]
    for k in range(hops):
        parts, (w_down_here, gate_up) = tick(
            [(hop, attn_in[-1]), (hop, out_rows[-1])], (w_down_here, gate_up)
        )
        attn_in.append(parts[0])
        out_rows.append(parts[1])
    attn_in = placed(attn_in, sources)
    w_out_all = gather_rows(placed(out_rows, sources)).reshape(width, width)

    gate_up = exchange(gate_up)
    w_gate_up = gather_rows(gate_up).reshape(width, 2 * units)
    cot = [after(cotangent, gate_up)]

    docs = doc_number(jnp.arange(nz * t, dtype=jnp.int32), jnp.cumsum(lengths[0]))
    docs_down, docs_across = docs[:, None], docs[None, :]
    def cot_hop():
        return [(hop, cot[-1])] if len(cot) < nz else []

    three = dot(attn_in, w_qkv).astype(bf16)
    attended = local_kernel(attention_kernel, feats, three, docs_down, docs_across)
    part, attended = tick(cot_hop(), attended)
    cot += part
    (attended_b,), _ = tick([(exchange, attended.reshape(nz, t, feats))])
    attended_b = regrouped(attended_b.transpose(1, 0, 2).reshape(t, width), n)
    middle = inputs + dot(attended_b, w_out_all)
    normed_ffn, inverse_ffn = rms_parts(middle)
    normed_ffn_b = regrouped((normed_ffn * norm_ffn).astype(bf16), n)
    part, normed_ffn_b = tick(cot_hop(), normed_ffn_b)
    cot += part

    ffn_in = [normed_ffn_b]
    for _ in range(hops):
        (part, *more), _ = tick([(hop, ffn_in[-1])] + cot_hop())
        ffn_in.append(part)
        cot += more

    def ring_first(partials):
        return hop(partials[1 % nz].astype(bf16))

    hidden, grad_gate_up, left, right = feed(ffn_in, cot, sources, w_gate_up, w_down_here, tile)
    line = Line()

    def other_half(x, y):
        return rows_product(x, y, 1 - core, me, n, "other")

    def core_swap(parts):
        return [cross(part, "c", 1) for part in parts]

    def gu_piece(first, last):
        return lambda x, came: rows_product(
            x, grad_gate_up, core, me, n, "cut", came, first, last
        )

    def summed_piece(own, came):
        return line(lambda own, came: summed(own, *came).astype(bf16), own, came)

    def to_line_sum(x):
        return lax.psum_scatter(x, "z", scatter_dimension=0, tiled=True)

    grad_normed_ffn = to_line_sum(line(lambda x: dot_nt(x, w_gate_up).astype(bf16), grad_gate_up))
    gu_other = core_swap(line(other_half, left, grad_gate_up))
    down_own, down_other = line(lambda x, y: down_product(x, y, core, me, n), hidden, right)
    down_other = core_swap(down_other)
    first_own, *first_parts = line(gu_piece(0, cut), left, gu_other)
    first_came = plane_sent(first_parts, 1, n - 1)
    second_own, *second_parts = line(gu_piece(cut, 2 * units), left, gu_other)
    out_parts = line(lambda x: dot(x, w_down_here).astype(bf16), hidden)

    def ffn_back_piece(total):
        total = ungrouped(total.astype(f32), n)
        back, gain_part = norm_back(total, norm_ffn, normed_ffn, inverse_ffn)
        grad_middle = cotangent.astype(f32) + back
        return grad_middle, grad_middle.astype(bf16), gain_part

    grad_normed_ffn, first_came, first_parts = line.hold(grad_normed_ffn, first_came, first_parts)
    first_came = first_came + plane_sent(first_parts, n - 1, n)
    grad_middle, grad_branch_b, gain_ffn_part = line(ffn_back_piece, grad_normed_ffn)
    grad_att = exchange(line(lambda x: heads_product(x, w_out_all, n, nz), grad_branch_b))
    branch = lax.all_gather(grad_branch_b, "z", axis=0, tiled=True)
    down_sums = line(
        lambda own, came: [plus(x, y).astype(bf16) for x, y in zip(own, came, strict=True)][1:],
        down_own,
        down_other,
    )
    first_came, second_parts = line.hold(first_came, second_parts)
    second_came = plane_sent(second_parts, 1, n - 1)
    grad_first = summed_piece(first_own, first_came)
    second_came, second_parts = line.hold(second_came, second_parts)
    second_came = second_came + plane_sent(second_parts, n - 1, n)
    grad_three = line(
        lambda x: local_kernel(
            attention_back_kernel,
            3 * feats,
            three,
            x.reshape(nz * t, feats),
            docs_down,
            docs_across,
        ),
        grad_att,
    )
    grad_first = exchange(grad_first.reshape(nz, own_rows, cut))
    grad_normed_attn = to_line_sum(line(lambda x: dot_nt(x, w_qkv).astype(bf16), grad_three))
    qkv_other = core_swap(line(other_half, attn_in, grad_three))
    second_came, grad_first, out_parts = line.hold(second_came, grad_first, out_parts)
    out_total = to_line_sum(out_parts)
    qkv_own, *qkv_parts = line(
        lambda x, came: rows_product(x, grad_three, core, me, n, "cut", came), attn_in, qkv_other
    )
    qkv_came = plane_sent(qkv_parts, 1, n - 1)
    grad_second = summed_piece(second_own, second_came)
    grad_second = exchange(grad_second.reshape(nz, own_rows, 2 * units - cut))
    out_other = core_swap(line(other_half, attended, branch))
    qkv_came, qkv_parts, down_sums = line.hold(qkv_came, qkv_parts, down_sums)
    qkv_came = qkv_came + plane_sent(qkv_parts, n - 1, n)
    out_own, *out_sums = line(
        lambda x, y, came: rows_product(x, y, core, me, n, "cut", came), attended, branch, out_other
    )
    down_came = plane_sent(down_sums, 1, n - 1)

    def attn_norm_piece(total):
        total = ungrouped(total.astype(f32), n)
        back, gain_part = norm_back(total, norm_attn, normed_attn, inverse_attn)
        return grad_middle + back, jnp.stack([gain_part, gain_ffn_part])

    token_grad, gains = line(attn_norm_piece, grad_normed_attn)
    grad_second, qkv_came, out_sums = line.hold(grad_second, qkv_came, out_sums)
    grad_qkv = summed_piece(qkv_own, qkv_came)
    grad_qkv = exchange(grad_qkv.reshape(nz, own_rows, 3 * feats))
    out_sums = plane_sent(out_sums, 1, n)
    down_came, down_sums = line.hold(down_came, down_sums)
    down_came = down_came + plane_sent(down_sums, n - 1, n)
    grad_w_out = summed_piece(out_own, out_sums)
    grad_w_out = lax.ppermute(
        grad_w_out, ("p", "z"), [(i * nz + j, j * nz + i) for i in range(n) for j in range(nz)]
    )
    grad_w_gate, grad_w_up = line(lambda x, y: collect(x, y, pieces), grad_first, grad_second)
    grad_w_down = line(
        lambda own, other, came: summed(plus(own[0], other[0]), *came),
        down_own,
        down_other,
        down_came,
    )
    activations = (middle + out_total.astype(f32)).astype(bf16)
    for axis in ("c", "p", "z"):
        gains = paired_sum([gains, *spread_sums(gains, axis)])

    def three_piece(x):
        return [
            x[:, :, i * feats : (i + 1) * feats]
            .transpose(1, 0, 2)
            .reshape(own_rows, width)
            .astype(f32)
            for i in range(3)
        ]

    grad_w_query, grad_w_key, grad_w_value = line(three_piece, grad_qkv)
    grad_w_out = line(lambda x: x.astype(f32), grad_w_out)
    gains = gains + jnp.sum(line.token)
    grad_w_down = grad_w_down.astype(f32)
    return (
        activations,
        token_grad,
        gains[0],
        grad_w_query,
        grad_w_key,
        grad_w_value,
        grad_w_out,
        gains[1],
        grad_w_gate,
        grad_w_up,
        grad_w_down,
    )


def solution(mesh):
    dp, seq = mesh.shape["dp"], mesh.shape["seq"]
    grid = Mesh(mesh.devices.reshape(dp // 2, 2, seq), ALL)
    split = P(ALL, None)
    return jax.shard_map(
        body,
        mesh=grid,
        in_specs=(split, split, P(("p", "c"), None), P())
        + (split,) * 4
        + (P(),)
        + (split,) * 3,
        out_specs=(split, split, P(), split, split, split, split, P(), split, split, split),
        check_vma=False,
    )
```

```python
import functools
import math

import jax
import jax.numpy as jnp
from jax import lax
from jax.experimental import pallas as pl
from jax.experimental.pallas import tpu as pltpu
from jax.sharding import Mesh
from jax.sharding import PartitionSpec as P

HEADS = 16
HEAD = 128
WINDOW = 64
BLOCK = 128
PARTS = 1

ALL = ("p", "c", "z")
norm_eps = 1e-05
masked_score = -1e30
f32 = jnp.float32
bf16 = jnp.bfloat16


def dot(left, right, dims=((1,), (0,))):
    return lax.dot_general(left, right, (dims, ((), ())), preferred_element_type=f32)


def dot_nt(left, right):
    return dot(left, right, ((1,), (1,)))


def dot_tn(left, right):
    return dot(left, right, ((0,), (0,)))


def cross(x, axis, by):
    n = lax.axis_size(axis)
    return lax.ppermute(x, axis, [(i, i ^ by) for i in range(n)])


def ring_order(n):
    return list(range(1, n, 2)) + list(range(n - 2, -1, -2)) if n > 1 else [0]


def hop(x):
    n = lax.axis_size("z")
    order = ring_order(n)
    return lax.ppermute(x, "z", [(order[i], order[(i + 1) % n]) for i in range(n)])


def ring_sources(n):
    order = ring_order(n)
    spot = {place: at for at, place in enumerate(order)}
    return [[order[(spot[z] - k) % n] for k in range(n)] for z in range(n)]


def placed(parts, sources):
    out = jnp.zeros((len(parts),) + parts[0].shape, parts[0].dtype)
    for k, part in enumerate(parts):
        out = lax.dynamic_update_slice(out, part[None], (sources[k],) + (0,) * part.ndim)
    return out.reshape((-1,) + parts[0].shape[1:])


def gather_rows(x):
    return lax.all_gather(x, ("c", "p"), axis=0, tiled=False)


def indexed(x, at, axis):
    return lax.dynamic_index_in_dim(x, at, axis, keepdims=False)


def after(x, *others):
    return lax.optimization_barrier((x, others))[0]


def blocks_in_order(x, order):
    wide = x.shape[1] // len(order)
    return jnp.concatenate([x[:, i * wide : (i + 1) * wide] for i in order], axis=1)


def regrouped(x, n):
    return blocks_in_order(x, [2 * i + c for c in range(2) for i in range(n)])


def ungrouped(x, n):
    return blocks_in_order(x, [c * n + i for i in range(n) for c in range(2)])


def tick(jobs, also=()):
    operands = lax.optimization_barrier([operand for _, operand in jobs])
    results = [job(operand) for (job, _), operand in zip(jobs, operands, strict=True)]
    return lax.optimization_barrier((results, also))


def crossing(axis, by):
    return lambda x: cross(x, axis, by)


def exchange(x):
    return lax.all_to_all(x, "z", 0, 0, tiled=True)


def plus(kept, came):
    return kept.astype(f32) + came.astype(f32)


class Line:
    def __init__(self):
        self.token = lax.optimization_barrier(jnp.zeros((8, 128), f32))

    def hold(self, *values):
        values, self.token = lax.optimization_barrier((values, self.token))
        return values[0] if len(values) == 1 else values

    def __call__(self, piece, *values):
        values, self.token = lax.optimization_barrier((values, self.token))
        return self.hold(piece(*values))


def plane_sent(parts, first, last):
    return [cross(parts[by - 1], "p", by) for by in range(first, last)]


def summed(*parts):
    return sum(part.astype(f32) for part in parts)


def spread_sums(x, axis):
    return [cross(x, axis, by) for by in range(1, lax.axis_size(axis))]


def paired_sum(parts):
    while len(parts) > 1:
        parts = [parts[i] + parts[i + 1] for i in range(0, len(parts), 2)]
    return parts[0]


def doc_number(positions, doc_ends):
    return jnp.sum((positions[:, None] >= doc_ends[None, :]).astype(jnp.int32), axis=1)


def allowed_pairs(at, low, count, docs_down_ref, docs_across_ref):
    query_at = at + lax.broadcasted_iota(jnp.int32, (BLOCK, count), 0)
    key_at = low + lax.broadcasted_iota(jnp.int32, (BLOCK, count), 1)
    same = docs_down_ref[at : at + BLOCK, :] == docs_across_ref[:, low : low + count]
    return (key_at <= query_at) & (key_at > query_at - WINDOW) & same


def softmax(query, key, allowed):
    scores = jnp.where(allowed, dot_nt(query, key) * (1.0 / math.sqrt(HEAD)), masked_score)
    exped = jnp.exp(scores - jnp.max(scores, axis=-1, keepdims=True))
    return exped / jnp.sum(exped, axis=-1, keepdims=True)


def attention_kernel(qkv_ref, docs_down_ref, docs_across_ref, out_ref):
    length, width = out_ref.shape
    for at in range(0, length, BLOCK):
        low = max(0, at - BLOCK)
        allowed = allowed_pairs(at, low, at + BLOCK - low, docs_down_ref, docs_across_ref)
        for h in range(0, width, HEAD):
            query = qkv_ref[at : at + BLOCK, h : h + HEAD]
            key = qkv_ref[low : at + BLOCK, width + h : width + h + HEAD]
            value = qkv_ref[low : at + BLOCK, 2 * width + h : 2 * width + h + HEAD]
            probs = softmax(query, key, allowed)
            out_ref[at : at + BLOCK, h : h + HEAD] = dot(probs.astype(bf16), value).astype(bf16)


def attention_back_kernel(qkv_ref, grad_ref, docs_down_ref, docs_across_ref, out_ref):
    length, width = grad_ref.shape
    scale = 1.0 / math.sqrt(HEAD)
    pending = {}
    for at in range(0, length, BLOCK):
        low = max(0, at - BLOCK)
        allowed = allowed_pairs(at, low, at + BLOCK - low, docs_down_ref, docs_across_ref)
        for h in range(0, width, HEAD):
            query = qkv_ref[at : at + BLOCK, h : h + HEAD]
            key = qkv_ref[low : at + BLOCK, width + h : width + h + HEAD]
            value = qkv_ref[low : at + BLOCK, 2 * width + h : 2 * width + h + HEAD]
            grad = grad_ref[at : at + BLOCK, h : h + HEAD]
            probs = softmax(query, key, allowed)
            grad_probs = dot_nt(grad, value)
            inner = jnp.sum(probs * grad_probs, axis=-1, keepdims=True)
            grad_scores = (probs * (grad_probs - inner)).astype(bf16)
            out_ref[at : at + BLOCK, h : h + HEAD] = (dot(grad_scores, key) * scale).astype(bf16)
            grad_key = dot_tn(grad_scores, query) * scale
            grad_value = dot_tn(probs.astype(bf16), grad)
            if at > 0:
                before_key, before_value = pending[h]
                out_ref[low:at, width + h : width + h + HEAD] = (
                    before_key + grad_key[:BLOCK]
                ).astype(bf16)
                out_ref[low:at, 2 * width + h : 2 * width + h + HEAD] = (
                    before_value + grad_value[:BLOCK]
                ).astype(bf16)
            pending[h] = (grad_key[at - low :], grad_value[at - low :])
    for h, (last_key, last_value) in pending.items():
        out_ref[length - BLOCK :, width + h : width + h + HEAD] = last_key.astype(bf16)
        out_ref[length - BLOCK :, 2 * width + h : 2 * width + h + HEAD] = last_value.astype(bf16)


def local_kernel(kernel, columns, *args):
    length = args[0].shape[0]
    return pl.pallas_call(
        kernel,
        out_shape=jax.ShapeDtypeStruct((length, columns), bf16),
        in_specs=[pl.BlockSpec(memory_space=pltpu.VMEM)] * len(args),
        out_specs=pl.BlockSpec(memory_space=pltpu.VMEM),
        compiler_params=kernel_params(10),
        cost_estimate=kernel_cost(0),
    )(*args)


def unit_pieces(n, nz, block, tile):
    pieces = []
    for j in range(2 * n * nz):
        start = ((j // nz % 2) * n + j // nz // 2) * block
        at = start
        while at < start + block:
            end = min(start + block, (at // tile + 1) * tile)
            column = at // tile * 2 * tile + at % tile
            pieces.append((j * block + at - start, j % nz, column, column + tile, end - at))
            at = end
    return pieces


def spread_kernel(pieces, gate_ref, up_ref, out_ref):
    for stored, z, gate_at, up_at, size in pieces:
        out_ref[z, :, gate_at : gate_at + size] = gate_ref[:, stored : stored + size]
        out_ref[z, :, up_at : up_at + size] = up_ref[:, stored : stored + size]


def collect_kernel(pieces, cut, first_ref, second_ref, gate_ref, up_ref):
    for stored, z, gate_at, up_at, size in pieces:
        for at, ref in ((gate_at, gate_ref), (up_at, up_ref)):
            inside = min(max(cut - at, 0), size)
            for source, low, start, count in (
                (first_ref, at, stored, inside),
                (second_ref, at + inside - cut, stored + inside, size - inside),
            ):
                if count:
                    ref[:, start : start + count] = source[z, :, low : low + count].astype(f32)


def spread(gate, up, nz, pieces):
    rows, wide = gate.shape
    return pl.pallas_call(
        functools.partial(spread_kernel, pieces),
        out_shape=jax.ShapeDtypeStruct((nz, rows, 2 * wide // nz), gate.dtype),
        name="spread_units",
    )(gate, up)


def collect(first, second, pieces):
    nz, rows, cut = first.shape
    wide = nz * (cut + second.shape[2]) // 2
    return pl.pallas_call(
        functools.partial(collect_kernel, pieces, cut),
        out_shape=[jax.ShapeDtypeStruct((rows, wide), f32)] * 2,
        name="collect_units",
    )(first, second)


def units_back(gate, up, grad_hidden):
    sig = jax.nn.sigmoid(gate)
    silu = gate * sig
    return (
        (silu * up).astype(bf16),
        (grad_hidden * up * sig * (1.0 + gate * (1.0 - sig))).astype(bf16),
        (grad_hidden * silu).astype(bf16),
    )


def feed_kernel(nz, places_ref, *refs):
    lefts, rights = refs[:nz], refs[nz : 2 * nz]
    gate_up_ref, down_ref, hidden_ref, grad_ref, left_ref, right_ref = refs[2 * nz :]
    t, tile = lefts[0].shape[0], down_ref.shape[0]

    @pl.when(pl.program_id(0) == 0)
    def _():
        for k in range(nz):
            start = pl.multiple_of(places_ref[k] * t, t)
            left_ref[pl.ds(start, t), :] = lefts[k][...]
            right_ref[pl.ds(start, t), :] = rights[k][...]

    both = dot(left_ref[...], gate_up_ref[...])
    grad_hidden = dot_nt(right_ref[...], down_ref[...])
    hidden, grad_gate, grad_up = units_back(both[:, :tile], both[:, tile:], grad_hidden)
    hidden_ref[...] = hidden
    grad_ref[:, :tile] = grad_gate
    grad_ref[:, tile:] = grad_up


def feed(lefts, rights, places, w_gate_up, w_down, tile):
    nz, (t, width) = len(lefts), lefts[0].shape
    units = w_down.shape[0]
    if tile != 128:
        left, right = placed(lefts, places), placed(rights, places)
        both = dot(left, w_gate_up)
        grad_hidden = dot_nt(right, w_down)
        hidden, grad_gate, grad_up = units_back(both[:, :units], both[:, units:], grad_hidden)
        return hidden, jnp.concatenate([grad_gate, grad_up], axis=1), left, right
    rows = nz * t
    whole = pl.BlockSpec((t, width), lambda i, at: (0, 0))
    every = pl.BlockSpec((rows, width), lambda i, at: (0, 0))
    return pl.pallas_call(
        functools.partial(feed_kernel, nz),
        grid_spec=pltpu.PrefetchScalarGridSpec(
            num_scalar_prefetch=1,
            grid=(units // tile,),
            in_specs=[whole] * (2 * nz)
            + [
                pl.BlockSpec((width, 2 * tile), lambda i, at: (0, i)),
                pl.BlockSpec((tile, width), lambda i, at: (i, 0)),
            ],
            out_specs=[
                pl.BlockSpec((rows, tile), lambda i, at: (0, i)),
                pl.BlockSpec((rows, 2 * tile), lambda i, at: (0, i)),
                every,
                every,
            ],
        ),
        out_shape=[
            jax.ShapeDtypeStruct((rows, units), bf16),
            jax.ShapeDtypeStruct((rows, 2 * units), bf16),
            jax.ShapeDtypeStruct((rows, width), bf16),
            jax.ShapeDtypeStruct((rows, width), bf16),
        ],
        compiler_params=kernel_params(60),
        cost_estimate=kernel_cost(18),
        name="feed_units",
    )(places, *lefts, *rights, w_gate_up, w_down)


def kernel_cost(us):
    return pl.CostEstimate(flops=int(us * 1.15e9 * 0.5), bytes_accessed=0, transcendentals=0)


def kernel_params(mib):
    return pltpu.CompilerParams(vmem_limit_bytes=mib * 1024 * 1024)


def tile_of(columns, most=1408):
    return max(tile for tile in range(128, most + 1, 128) if columns % tile == 0)


def rows_kernel(n, mode, at_ref, left_ref, right_ref, *refs):
    flip_ref, total_ref = refs[-2:]
    came, outs = (refs[:0], refs[:-2]) if mode == "other" else (refs[:PARTS], refs[PARTS:-2])

    @pl.when(pl.program_id(0) == 0)
    def _():
        flip_ref[...] = left_ref[...].T

    total = dot(flip_ref[...], right_ref[...])
    size = total.shape[0] // PARTS
    for k in range(PARTS):
        part = total[k * size : (k + 1) * size]
        if mode == "other":
            outs[k][...] = part.astype(bf16)
        else:
            part = (part + came[k][...].astype(f32)).astype(bf16)
            into = outs[0] if mode == "whole" else total_ref
            into[k * size : (k + 1) * size, :] = part
    if mode == "cut":
        rest = total.shape[0] // n
        for by in range(n):
            start = pl.multiple_of((at_ref[1] ^ by) * rest, rest)
            outs[by][...] = total_ref[pl.ds(start, rest), :]


def rows_product(left, right, half, me, n, mode, came=(), first=0, last=None):
    t, rows = left.shape[0], left.shape[1] // 2
    last = right.shape[1] if last is None else last
    tile = tile_of(math.gcd(last - first, first) if first else last)
    rest, columns, off = rows // n, last - first, first // tile
    at = jnp.stack([half, me]).astype(jnp.int32)
    outs, height = {"whole": (1, rows), "cut": (n, rest), "other": (PARTS, rows // PARTS)}[mode]
    return pl.pallas_call(
        functools.partial(rows_kernel, n, mode),
        grid_spec=pltpu.PrefetchScalarGridSpec(
            num_scalar_prefetch=1,
            grid=(columns // tile,),
            in_specs=[
                pl.BlockSpec((t, rows), lambda i, at: (0, at[0])),
                pl.BlockSpec((t, tile), lambda i, at: (0, i + off)),
            ]
            + [pl.BlockSpec((rows // PARTS, tile), lambda i, at: (0, i + off))] * len(came),
            out_specs=[pl.BlockSpec((height, tile), lambda i, at: (0, i))] * outs,
            scratch_shapes=[pltpu.VMEM((rows, t), bf16), pltpu.VMEM((rows, tile), bf16)],
        ),
        out_shape=[jax.ShapeDtypeStruct((height, columns), bf16)] * outs,
        compiler_params=kernel_params(60),
        cost_estimate=kernel_cost(6.5),
        name="rows_product",
    )(at, left, right, *came)


def down_kernel(n, at_ref, left_ref, right_ref, *refs):
    outs, flip_ref, total_ref = refs[:-2], refs[-2], refs[-1]
    rest = outs[0].shape[0]

    @pl.when(pl.program_id(0) == 0)
    def _():
        flip_ref[...] = left_ref[...].T

    total_ref[...] = dot(flip_ref[...], right_ref[...]).astype(bf16)
    for k, out_ref in enumerate(outs):
        half = at_ref[0] if k < n else 1 - at_ref[0]
        start = (half * n + (at_ref[1] ^ (k % n))) * rest
        out_ref[...] = total_ref[pl.ds(pl.multiple_of(start, math.gcd(rest, 16)), rest), :]


def down_product(left, right, core, me, n):
    t, rows = left.shape
    columns = right.shape[1]
    tile = tile_of(columns)
    rest = rows // (2 * n)
    if rest % 16:
        full = dot_tn(left, right).astype(bf16).reshape(2, n, rest, columns)
        parts = [indexed(indexed(full, at, 0), me ^ by, 0) for at in (core, 1 - core) for by in range(n)]
        return parts[:n], parts[n:]
    parts = pl.pallas_call(
        functools.partial(down_kernel, n),
        grid_spec=pltpu.PrefetchScalarGridSpec(
            num_scalar_prefetch=1,
            grid=(columns // tile,),
            in_specs=[
                pl.BlockSpec((t, rows), lambda i, at: (0, 0)),
                pl.BlockSpec((t, tile), lambda i, at: (0, i)),
            ],
            out_specs=[pl.BlockSpec((rest, tile), lambda i, at: (0, i))] * (2 * n),
            scratch_shapes=[pltpu.VMEM((rows, t), bf16), pltpu.VMEM((rows, tile), bf16)],
        ),
        out_shape=[jax.ShapeDtypeStruct((rest, columns), bf16)] * (2 * n),
        compiler_params=kernel_params(60),
        cost_estimate=kernel_cost(7),
        name="down_product",
    )(jnp.stack([core, me]).astype(jnp.int32), left, right)
    return parts[:n], parts[n:]


def chunks_kernel(transposed, at_ref, x_ref, w_ref, *refs):
    outs, total_ref = refs[:-1], refs[-1]
    t = outs[0].shape[0]
    total_ref[...] = (dot_nt if transposed else dot)(x_ref[...], w_ref[...])
    for k, out_ref in enumerate(outs):
        start = pl.multiple_of(at_ref[k] * t, t)
        out_ref[...] = total_ref[pl.ds(start, t), :].astype(out_ref.dtype)


def chunks_product(x, w, places, transposed):
    rows, depth = x.shape
    n, columns = places.shape[0], w.shape[0 if transposed else 1]
    tile = tile_of(columns)
    w_spec = (
        pl.BlockSpec((tile, depth), lambda i, at: (i, 0))
        if transposed
        else pl.BlockSpec((depth, tile), lambda i, at: (0, i))
    )
    return pl.pallas_call(
        functools.partial(chunks_kernel, transposed),
        grid_spec=pltpu.PrefetchScalarGridSpec(
            num_scalar_prefetch=1,
            grid=(columns // tile,),
            in_specs=[pl.BlockSpec((rows, depth), lambda i, at: (0, 0)), w_spec],
            out_specs=[pl.BlockSpec((rows // n, tile), lambda i, at: (0, i))] * n,
            scratch_shapes=[pltpu.VMEM((rows, tile), f32)],
        ),
        out_shape=[
            jax.ShapeDtypeStruct((rows // n, columns), bf16 if k == 1 % n else f32) for k in range(n)
        ],
        compiler_params=kernel_params(60),
        cost_estimate=kernel_cost(8),
        name="chunks_product",
    )(places, x, w)


def heads_kernel(x_ref, w_ref, out_ref):
    out_ref[0] = dot_nt(x_ref[...], w_ref[...]).astype(bf16)


def heads_product(x, w, n, nz):
    rows, depth = x.shape
    rest, feats = w.shape[0] // (2 * n), w.shape[0] // nz
    per = feats // rest

    def place(i):
        block = i % n * 2 + i // n
        return (block // per, 0, block % per)

    return pl.pallas_call(
        heads_kernel,
        grid=(2 * n,),
        in_specs=[
            pl.BlockSpec((rows, depth), lambda i: (0, 0)),
            pl.BlockSpec((rest, depth), lambda i: (i, 0)),
        ],
        out_specs=pl.BlockSpec((1, rows, rest), place),
        out_shape=jax.ShapeDtypeStruct((nz, rows, feats), bf16),
        compiler_params=kernel_params(60),
        cost_estimate=kernel_cost(0),
        name="heads_product",
    )(x, w)


def rms_parts(values):
    inverse = lax.rsqrt(jnp.mean(values * values, axis=1, keepdims=True) + norm_eps)
    return (values * inverse, inverse)


def norm_back(grad_normed, gain, normed, inverse):
    scaled = grad_normed * gain
    back = inverse * (scaled - normed * jnp.mean(scaled * normed, axis=1, keepdims=True))
    return (back, jnp.sum(grad_normed * normed, axis=0))


def body(
    tokens,
    cotangent,
    lengths,
    norm_attn,
    w_query,
    w_key,
    w_value,
    w_out,
    norm_ffn,
    w_gate,
    w_up,
    w_down,
):
    t, width = tokens.shape
    own_rows, hidden_width = w_gate.shape
    nz = lax.axis_size("z")
    groups = lax.axis_size("p") * 2
    sources = jnp.asarray(ring_sources(nz), jnp.int32)[lax.axis_index("z")]
    feats = width // nz
    block = hidden_width // (groups * nz)
    units = groups * block
    group_rows = nz * own_rows

    n = lax.axis_size("p")
    me, core = lax.axis_index("p"), lax.axis_index("c")
    hops = nz - 1

    inputs = tokens.astype(f32)
    normed_attn, inverse_attn = rms_parts(inputs)
    normed_attn_b = regrouped((normed_attn * norm_attn).astype(bf16), n)

    w_down_here = gather_rows(w_down).reshape(units, width)
    qkv = jnp.concatenate(
        [w.reshape(own_rows, nz, feats) for w in (w_query, w_key, w_value)], axis=2
    ).transpose(1, 0, 2)
    qkv = exchange(qkv)
    w_qkv = gather_rows(qkv).reshape(width, 3 * feats)

    tile = 128 if units % 128 == 0 else units
    cut = -(-units // 256) * 256
    pieces = unit_pieces(n, nz, block, tile)
    gate_up = spread(w_gate, w_up, nz, pieces)
    def laid(whole, part, k):
        return lax.dynamic_update_slice(whole, part, (sources[k] * part.shape[0], 0))

    came, out_came = normed_attn_b, w_out
    attn_in = laid(jnp.zeros((nz * t, width), bf16), came, 0)
    out_rows = laid(jnp.zeros((nz * own_rows, width), bf16), out_came, 0)
    for k in range(hops):
        (came, out_came), (w_down_here, gate_up, attn_in, out_rows) = tick(
            [(hop, came), (hop, out_came)], (w_down_here, gate_up, attn_in, out_rows)
        )
        attn_in, out_rows = laid(attn_in, came, k + 1), laid(out_rows, out_came, k + 1)
    w_out_all = gather_rows(out_rows.reshape(nz, own_rows, width)).reshape(width, width)

    gate_up = exchange(gate_up)
    w_gate_up = gather_rows(gate_up).reshape(width, 2 * units)
    cot = [after(cotangent, gate_up)]

    docs = doc_number(jnp.arange(nz * t, dtype=jnp.int32), jnp.cumsum(lengths[0]))
    docs_down, docs_across = docs[:, None], docs[None, :]
    def cot_hop():
        return [(hop, cot[-1])] if len(cot) < nz else []

    three = dot(attn_in, w_qkv).astype(bf16)
    attended = local_kernel(attention_kernel, feats, three, docs_down, docs_across)
    part, attended = tick(cot_hop(), attended)
    cot += part
    (attended_b,), _ = tick([(exchange, attended.reshape(nz, t, feats))])
    attended_b = regrouped(attended_b.transpose(1, 0, 2).reshape(t, width), n)
    middle = inputs + dot(attended_b, w_out_all)
    normed_ffn, inverse_ffn = rms_parts(middle)
    normed_ffn_b = regrouped((normed_ffn * norm_ffn).astype(bf16), n)
    part, normed_ffn_b = tick(cot_hop(), normed_ffn_b)
    cot += part

    ffn_in = [normed_ffn_b]
    for _ in range(hops):
        (part, *more), _ = tick([(hop, ffn_in[-1])] + cot_hop())
        ffn_in.append(part)
        cot += more

    def ring_first(partials):
        return hop(partials[1 % nz].astype(bf16))

    hidden, grad_gate_up, left, right = feed(ffn_in, cot, sources, w_gate_up, w_down_here, tile)
    line = Line()

    def other_half(x, y):
        return rows_product(x, y, 1 - core, me, n, "other")

    def core_swap(parts):
        return [cross(part, "c", 1) for part in parts]

    def gu_piece(first, last):
        return lambda x, came: rows_product(
            x, grad_gate_up, core, me, n, "cut", came, first, last
        )

    def summed_piece(own, came):
        return line(lambda own, came: summed(own, *came).astype(bf16), own, came)

    def to_line_sum(x):
        return lax.psum_scatter(x, "z", scatter_dimension=0, tiled=True)

    grad_normed_ffn = to_line_sum(line(lambda x: dot_nt(x, w_gate_up).astype(bf16), grad_gate_up))
    gu_other = core_swap(line(other_half, left, grad_gate_up))
    down_own, down_other = line(lambda x, y: down_product(x, y, core, me, n), hidden, right)
    down_other = core_swap(down_other)
    first_own, *first_parts = line(gu_piece(0, cut), left, gu_other)
    first_came = plane_sent(first_parts, 1, n - 1)
    second_own, *second_parts = line(gu_piece(cut, 2 * units), left, gu_other)
    out_parts = line(lambda x: dot(x, w_down_here).astype(bf16), hidden)

    def ffn_back_piece(total):
        total = ungrouped(total.astype(f32), n)
        back, gain_part = norm_back(total, norm_ffn, normed_ffn, inverse_ffn)
        grad_middle = cotangent.astype(f32) + back
        return grad_middle, grad_middle.astype(bf16), gain_part

    grad_normed_ffn, first_came, first_parts = line.hold(grad_normed_ffn, first_came, first_parts)
    first_came = first_came + plane_sent(first_parts, n - 1, n)
    grad_middle, grad_branch_b, gain_ffn_part = line(ffn_back_piece, grad_normed_ffn)
    grad_att = exchange(line(lambda x: heads_product(x, w_out_all, n, nz), grad_branch_b))
    branch = lax.all_gather(grad_branch_b, "z", axis=0, tiled=True)
    down_sums = line(
        lambda own, came: [plus(x, y).astype(bf16) for x, y in zip(own, came, strict=True)][1:],
        down_own,
        down_other,
    )
    first_came, second_parts = line.hold(first_came, second_parts)
    second_came = plane_sent(second_parts, 1, n - 1)
    grad_first = summed_piece(first_own, first_came)
    second_came, second_parts = line.hold(second_came, second_parts)
    second_came = second_came + plane_sent(second_parts, n - 1, n)
    grad_three = line(
        lambda x: local_kernel(
            attention_back_kernel,
            3 * feats,
            three,
            x.reshape(nz * t, feats),
            docs_down,
            docs_across,
        ),
        grad_att,
    )
    grad_first = exchange(grad_first.reshape(nz, own_rows, cut))
    grad_normed_attn = to_line_sum(line(lambda x: dot_nt(x, w_qkv).astype(bf16), grad_three))
    qkv_other = core_swap(line(other_half, attn_in, grad_three))
    second_came = line.hold(second_came)
    qkv_own, *qkv_parts = line(
        lambda x, came: rows_product(x, grad_three, core, me, n, "cut", came), attn_in, qkv_other
    )
    qkv_came = plane_sent(qkv_parts, 1, n - 1)
    qkv_came, qkv_parts = line.hold(qkv_came, qkv_parts)
    qkv_came = qkv_came + plane_sent(qkv_parts, n - 1, n)
    grad_first, out_parts = line.hold(grad_first, out_parts)
    out_total = to_line_sum(out_parts)
    grad_second = summed_piece(second_own, second_came)
    grad_second = exchange(grad_second.reshape(nz, own_rows, 2 * units - cut))
    out_other = core_swap(line(other_half, attended, branch))
    qkv_came, down_sums = line.hold(qkv_came, down_sums)
    out_own, *out_sums = line(
        lambda x, y, came: rows_product(x, y, core, me, n, "cut", came), attended, branch, out_other
    )
    down_came = plane_sent(down_sums, 1, n - 1)
    grad_qkv = summed_piece(qkv_own, qkv_came)
    grad_second = line.hold(grad_second)
    grad_qkv = exchange(grad_qkv.reshape(nz, own_rows, 3 * feats))

    def attn_norm_piece(total):
        total = ungrouped(total.astype(f32), n)
        back, gain_part = norm_back(total, norm_attn, normed_attn, inverse_attn)
        return grad_middle + back, jnp.stack([gain_part, gain_ffn_part])

    token_grad, gains = line(attn_norm_piece, grad_normed_attn)
    out_sums = line.hold(out_sums)
    out_sums = plane_sent(out_sums, 1, n)
    down_came, down_sums = line.hold(down_came, down_sums)
    down_came = down_came + plane_sent(down_sums, n - 1, n)
    grad_w_out = summed_piece(out_own, out_sums)
    grad_w_out = lax.ppermute(
        grad_w_out, ("p", "z"), [(i * nz + j, j * nz + i) for i in range(n) for j in range(nz)]
    )
    def three_piece(x):
        return [
            x[:, :, i * feats : (i + 1) * feats]
            .transpose(1, 0, 2)
            .reshape(own_rows, width)
            .astype(f32)
            for i in range(3)
        ]

    grad_w_query, grad_w_key, grad_w_value = line(three_piece, grad_qkv)

    grad_w_gate, grad_w_up = line(lambda x, y: collect(x, y, pieces), grad_first, grad_second)
    grad_w_down = line(
        lambda own, other, came: summed(plus(own[0], other[0]), *came),
        down_own,
        down_other,
        down_came,
    )
    activations = (middle + out_total.astype(f32)).astype(bf16)
    for axis in ("c", "p", "z"):
        gains = paired_sum([gains, *spread_sums(gains, axis)])
    grad_w_out = line(lambda x: x.astype(f32), grad_w_out)
    gains = gains + jnp.sum(line.token)
    grad_w_down = grad_w_down.astype(f32)
    return (
        activations,
        token_grad,
        gains[0],
        grad_w_query,
        grad_w_key,
        grad_w_value,
        grad_w_out,
        gains[1],
        grad_w_gate,
        grad_w_up,
        grad_w_down,
    )


def solution(mesh):
    dp, seq = mesh.shape["dp"], mesh.shape["seq"]
    grid = Mesh(mesh.devices.reshape(dp // 2, 2, seq), ALL)
    split = P(ALL, None)
    return jax.shard_map(
        body,
        mesh=grid,
        in_specs=(split, split, P(("p", "c"), None), P())
        + (split,) * 4
        + (P(),)
        + (split,) * 3,
        out_specs=(split, split, P(), split, split, split, split, P(), split, split, split),
        check_vma=False,
    )
```

```python
import functools
import math

import jax
import jax.numpy as jnp
from jax import lax
from jax.experimental import pallas as pl
from jax.experimental.pallas import tpu as pltpu
from jax.sharding import Mesh
from jax.sharding import PartitionSpec as P

HEADS = 16
HEAD = 128
WINDOW = 64
BLOCK = 128
PARTS = 1

ALL = ("p", "c", "z")
norm_eps = 1e-05
masked_score = -1e30
f32 = jnp.float32
bf16 = jnp.bfloat16


def dot(left, right, dims=((1,), (0,))):
    return lax.dot_general(left, right, (dims, ((), ())), preferred_element_type=f32)


def dot_nt(left, right):
    return dot(left, right, ((1,), (1,)))


def dot_tn(left, right):
    return dot(left, right, ((0,), (0,)))


def cross(x, axis, by):
    n = lax.axis_size(axis)
    return lax.ppermute(x, axis, [(i, i ^ by) for i in range(n)])


def ring_order(n):
    return list(range(1, n, 2)) + list(range(n - 2, -1, -2)) if n > 1 else [0]


def hop(x):
    n = lax.axis_size("z")
    order = ring_order(n)
    return lax.ppermute(x, "z", [(order[i], order[(i + 1) % n]) for i in range(n)])


def ring_sources(n):
    order = ring_order(n)
    spot = {place: at for at, place in enumerate(order)}
    return [[order[(spot[z] - k) % n] for k in range(n)] for z in range(n)]


def placed(parts, sources):
    out = jnp.zeros((len(parts),) + parts[0].shape, parts[0].dtype)
    for k, part in enumerate(parts):
        out = lax.dynamic_update_slice(out, part[None], (sources[k],) + (0,) * part.ndim)
    return out.reshape((-1,) + parts[0].shape[1:])


def gather_rows(x):
    return lax.all_gather(x, ("c", "p"), axis=0, tiled=False)


def indexed(x, at, axis):
    return lax.dynamic_index_in_dim(x, at, axis, keepdims=False)


def after(x, *others):
    return lax.optimization_barrier((x, others))[0]


def blocks_in_order(x, order):
    wide = x.shape[1] // len(order)
    return jnp.concatenate([x[:, i * wide : (i + 1) * wide] for i in order], axis=1)


def regrouped(x, n):
    return blocks_in_order(x, [2 * i + c for c in range(2) for i in range(n)])


def ungrouped(x, n):
    return blocks_in_order(x, [c * n + i for i in range(n) for c in range(2)])


def tick(jobs, also=()):
    operands = lax.optimization_barrier([operand for _, operand in jobs])
    results = [job(operand) for (job, _), operand in zip(jobs, operands, strict=True)]
    return lax.optimization_barrier((results, also))


def crossing(axis, by):
    return lambda x: cross(x, axis, by)


def exchange(x):
    return lax.all_to_all(x, "z", 0, 0, tiled=True)


def plus(kept, came):
    return kept.astype(f32) + came.astype(f32)


class Line:
    def __init__(self):
        self.token = lax.optimization_barrier(jnp.zeros((8, 128), f32))

    def hold(self, *values):
        values, self.token = lax.optimization_barrier((values, self.token))
        return values[0] if len(values) == 1 else values

    def __call__(self, piece, *values):
        values, self.token = lax.optimization_barrier((values, self.token))
        return self.hold(piece(*values))


def plane_sent(parts, first, last):
    return [cross(parts[by - 1], "p", by) for by in range(first, last)]


def summed(*parts):
    return sum(part.astype(f32) for part in parts)


def spread_sums(x, axis):
    return [cross(x, axis, by) for by in range(1, lax.axis_size(axis))]


def paired_sum(parts):
    while len(parts) > 1:
        parts = [parts[i] + parts[i + 1] for i in range(0, len(parts), 2)]
    return parts[0]


def doc_number(positions, doc_ends):
    return jnp.sum((positions[:, None] >= doc_ends[None, :]).astype(jnp.int32), axis=1)


def allowed_pairs(at, low, count, docs_down_ref, docs_across_ref):
    query_at = at + lax.broadcasted_iota(jnp.int32, (BLOCK, count), 0)
    key_at = low + lax.broadcasted_iota(jnp.int32, (BLOCK, count), 1)
    same = docs_down_ref[at : at + BLOCK, :] == docs_across_ref[:, low : low + count]
    return (key_at <= query_at) & (key_at > query_at - WINDOW) & same


def softmax(query, key, allowed):
    scores = jnp.where(allowed, dot_nt(query, key) * (1.0 / math.sqrt(HEAD)), masked_score)
    exped = jnp.exp(scores - jnp.max(scores, axis=-1, keepdims=True))
    return exped / jnp.sum(exped, axis=-1, keepdims=True)


def attention_kernel(qkv_ref, docs_down_ref, docs_across_ref, out_ref):
    length, width = out_ref.shape
    for at in range(0, length, BLOCK):
        low = max(0, at - BLOCK)
        allowed = allowed_pairs(at, low, at + BLOCK - low, docs_down_ref, docs_across_ref)
        for h in range(0, width, HEAD):
            query = qkv_ref[at : at + BLOCK, h : h + HEAD]
            key = qkv_ref[low : at + BLOCK, width + h : width + h + HEAD]
            value = qkv_ref[low : at + BLOCK, 2 * width + h : 2 * width + h + HEAD]
            probs = softmax(query, key, allowed)
            out_ref[at : at + BLOCK, h : h + HEAD] = dot(probs.astype(bf16), value).astype(bf16)


def attention_back_kernel(qkv_ref, grad_ref, docs_down_ref, docs_across_ref, out_ref):
    length, width = grad_ref.shape
    scale = 1.0 / math.sqrt(HEAD)
    pending = {}
    for at in range(0, length, BLOCK):
        low = max(0, at - BLOCK)
        allowed = allowed_pairs(at, low, at + BLOCK - low, docs_down_ref, docs_across_ref)
        for h in range(0, width, HEAD):
            query = qkv_ref[at : at + BLOCK, h : h + HEAD]
            key = qkv_ref[low : at + BLOCK, width + h : width + h + HEAD]
            value = qkv_ref[low : at + BLOCK, 2 * width + h : 2 * width + h + HEAD]
            grad = grad_ref[at : at + BLOCK, h : h + HEAD]
            probs = softmax(query, key, allowed)
            grad_probs = dot_nt(grad, value)
            inner = jnp.sum(probs * grad_probs, axis=-1, keepdims=True)
            grad_scores = (probs * (grad_probs - inner)).astype(bf16)
            out_ref[at : at + BLOCK, h : h + HEAD] = (dot(grad_scores, key) * scale).astype(bf16)
            grad_key = dot_tn(grad_scores, query) * scale
            grad_value = dot_tn(probs.astype(bf16), grad)
            if at > 0:
                before_key, before_value = pending[h]
                out_ref[low:at, width + h : width + h + HEAD] = (
                    before_key + grad_key[:BLOCK]
                ).astype(bf16)
                out_ref[low:at, 2 * width + h : 2 * width + h + HEAD] = (
                    before_value + grad_value[:BLOCK]
                ).astype(bf16)
            pending[h] = (grad_key[at - low :], grad_value[at - low :])
    for h, (last_key, last_value) in pending.items():
        out_ref[length - BLOCK :, width + h : width + h + HEAD] = last_key.astype(bf16)
        out_ref[length - BLOCK :, 2 * width + h : 2 * width + h + HEAD] = last_value.astype(bf16)


def local_kernel(kernel, columns, *args):
    length = args[0].shape[0]
    return pl.pallas_call(
        kernel,
        out_shape=jax.ShapeDtypeStruct((length, columns), bf16),
        in_specs=[pl.BlockSpec(memory_space=pltpu.VMEM)] * len(args),
        out_specs=pl.BlockSpec(memory_space=pltpu.VMEM),
        compiler_params=kernel_params(10),
        cost_estimate=kernel_cost(0),
    )(*args)


def unit_pieces(n, nz, block, tile):
    pieces = []
    for j in range(2 * n * nz):
        start = ((j // nz % 2) * n + j // nz // 2) * block
        at = start
        while at < start + block:
            end = min(start + block, (at // tile + 1) * tile)
            column = at // tile * 2 * tile + at % tile
            pieces.append((j * block + at - start, j % nz, column, column + tile, end - at))
            at = end
    return pieces


def spread_kernel(pieces, gate_ref, up_ref, out_ref):
    for stored, z, gate_at, up_at, size in pieces:
        out_ref[z, :, gate_at : gate_at + size] = gate_ref[:, stored : stored + size]
        out_ref[z, :, up_at : up_at + size] = up_ref[:, stored : stored + size]


def collect_kernel(pieces, cut, first_ref, second_ref, gate_ref, up_ref):
    for stored, z, gate_at, up_at, size in pieces:
        for at, ref in ((gate_at, gate_ref), (up_at, up_ref)):
            inside = min(max(cut - at, 0), size)
            for source, low, start, count in (
                (first_ref, at, stored, inside),
                (second_ref, at + inside - cut, stored + inside, size - inside),
            ):
                if count:
                    ref[:, start : start + count] = source[z, :, low : low + count].astype(f32)


def spread(gate, up, nz, pieces):
    rows, wide = gate.shape
    return pl.pallas_call(
        functools.partial(spread_kernel, pieces),
        out_shape=jax.ShapeDtypeStruct((nz, rows, 2 * wide // nz), gate.dtype),
        name="spread_units",
    )(gate, up)


def collect(first, second, pieces):
    nz, rows, cut = first.shape
    wide = nz * (cut + second.shape[2]) // 2
    return pl.pallas_call(
        functools.partial(collect_kernel, pieces, cut),
        out_shape=[jax.ShapeDtypeStruct((rows, wide), f32)] * 2,
        name="collect_units",
    )(first, second)


def units_back(gate, up, grad_hidden):
    sig = jax.nn.sigmoid(gate)
    silu = gate * sig
    return (
        (silu * up).astype(bf16),
        (grad_hidden * up * sig * (1.0 + gate * (1.0 - sig))).astype(bf16),
        (grad_hidden * silu).astype(bf16),
    )


def feed_kernel(nz, places_ref, *refs):
    lefts, rights = refs[:nz], refs[nz : 2 * nz]
    gate_up_ref, down_ref, hidden_ref, grad_ref, left_ref, right_ref = refs[2 * nz :]
    t, tile = lefts[0].shape[0], down_ref.shape[0]

    @pl.when(pl.program_id(0) == 0)
    def _():
        for k in range(nz):
            start = pl.multiple_of(places_ref[k] * t, t)
            left_ref[pl.ds(start, t), :] = lefts[k][...]
            right_ref[pl.ds(start, t), :] = rights[k][...]

    both = dot(left_ref[...], gate_up_ref[...])
    grad_hidden = dot_nt(right_ref[...], down_ref[...])
    hidden, grad_gate, grad_up = units_back(both[:, :tile], both[:, tile:], grad_hidden)
    hidden_ref[...] = hidden
    grad_ref[:, :tile] = grad_gate
    grad_ref[:, tile:] = grad_up


def feed(lefts, rights, places, w_gate_up, w_down, tile):
    nz, (t, width) = len(lefts), lefts[0].shape
    units = w_down.shape[0]
    if tile != 128:
        left, right = placed(lefts, places), placed(rights, places)
        both = dot(left, w_gate_up)
        grad_hidden = dot_nt(right, w_down)
        hidden, grad_gate, grad_up = units_back(both[:, :units], both[:, units:], grad_hidden)
        return hidden, jnp.concatenate([grad_gate, grad_up], axis=1), left, right
    rows = nz * t
    whole = pl.BlockSpec((t, width), lambda i, at: (0, 0))
    every = pl.BlockSpec((rows, width), lambda i, at: (0, 0))
    return pl.pallas_call(
        functools.partial(feed_kernel, nz),
        grid_spec=pltpu.PrefetchScalarGridSpec(
            num_scalar_prefetch=1,
            grid=(units // tile,),
            in_specs=[whole] * (2 * nz)
            + [
                pl.BlockSpec((width, 2 * tile), lambda i, at: (0, i)),
                pl.BlockSpec((tile, width), lambda i, at: (i, 0)),
            ],
            out_specs=[
                pl.BlockSpec((rows, tile), lambda i, at: (0, i)),
                pl.BlockSpec((rows, 2 * tile), lambda i, at: (0, i)),
                every,
                every,
            ],
        ),
        out_shape=[
            jax.ShapeDtypeStruct((rows, units), bf16),
            jax.ShapeDtypeStruct((rows, 2 * units), bf16),
            jax.ShapeDtypeStruct((rows, width), bf16),
            jax.ShapeDtypeStruct((rows, width), bf16),
        ],
        compiler_params=kernel_params(60),
        cost_estimate=kernel_cost(18),
        name="feed_units",
    )(places, *lefts, *rights, w_gate_up, w_down)


def kernel_cost(us):
    return pl.CostEstimate(flops=int(us * 1.15e9 * 0.5), bytes_accessed=0, transcendentals=0)


def kernel_params(mib):
    return pltpu.CompilerParams(vmem_limit_bytes=mib * 1024 * 1024)


def tile_of(columns, most=1408):
    return max(tile for tile in range(128, most + 1, 128) if columns % tile == 0)


def rows_kernel(n, mode, at_ref, left_ref, right_ref, *refs):
    flip_ref, total_ref = refs[-2:]
    came, outs = (refs[:0], refs[:-2]) if mode == "other" else (refs[:PARTS], refs[PARTS:-2])

    @pl.when(pl.program_id(0) == 0)
    def _():
        flip_ref[...] = left_ref[...].T

    total = dot(flip_ref[...], right_ref[...])
    size = total.shape[0] // PARTS
    for k in range(PARTS):
        part = total[k * size : (k + 1) * size]
        if mode == "other":
            outs[k][...] = part.astype(bf16)
        else:
            part = (part + came[k][...].astype(f32)).astype(bf16)
            into = outs[0] if mode == "whole" else total_ref
            into[k * size : (k + 1) * size, :] = part
    if mode == "cut":
        rest = total.shape[0] // n
        for by in range(n):
            start = pl.multiple_of((at_ref[1] ^ by) * rest, rest)
            outs[by][...] = total_ref[pl.ds(start, rest), :]


def rows_product(left, right, half, me, n, mode, came=(), first=0, last=None):
    t, rows = left.shape[0], left.shape[1] // 2
    last = right.shape[1] if last is None else last
    tile = tile_of(math.gcd(last - first, first) if first else last)
    rest, columns, off = rows // n, last - first, first // tile
    at = jnp.stack([half, me]).astype(jnp.int32)
    outs, height = {"whole": (1, rows), "cut": (n, rest), "other": (PARTS, rows // PARTS)}[mode]
    return pl.pallas_call(
        functools.partial(rows_kernel, n, mode),
        grid_spec=pltpu.PrefetchScalarGridSpec(
            num_scalar_prefetch=1,
            grid=(columns // tile,),
            in_specs=[
                pl.BlockSpec((t, rows), lambda i, at: (0, at[0])),
                pl.BlockSpec((t, tile), lambda i, at: (0, i + off)),
            ]
            + [pl.BlockSpec((rows // PARTS, tile), lambda i, at: (0, i + off))] * len(came),
            out_specs=[pl.BlockSpec((height, tile), lambda i, at: (0, i))] * outs,
            scratch_shapes=[pltpu.VMEM((rows, t), bf16), pltpu.VMEM((rows, tile), bf16)],
        ),
        out_shape=[jax.ShapeDtypeStruct((height, columns), bf16)] * outs,
        compiler_params=kernel_params(60),
        cost_estimate=kernel_cost(6.5),
        name="rows_product",
    )(at, left, right, *came)


def down_kernel(n, at_ref, left_ref, right_ref, *refs):
    outs, flip_ref, total_ref = refs[:-2], refs[-2], refs[-1]
    rest = outs[0].shape[0]

    @pl.when(pl.program_id(0) == 0)
    def _():
        flip_ref[...] = left_ref[...].T

    total_ref[...] = dot(flip_ref[...], right_ref[...]).astype(bf16)
    for k, out_ref in enumerate(outs):
        half = at_ref[0] if k < n else 1 - at_ref[0]
        start = (half * n + (at_ref[1] ^ (k % n))) * rest
        out_ref[...] = total_ref[pl.ds(pl.multiple_of(start, math.gcd(rest, 16)), rest), :]


def down_product(left, right, core, me, n):
    t, rows = left.shape
    columns = right.shape[1]
    tile = tile_of(columns)
    rest = rows // (2 * n)
    if rest % 16:
        full = dot_tn(left, right).astype(bf16).reshape(2, n, rest, columns)
        parts = [indexed(indexed(full, at, 0), me ^ by, 0) for at in (core, 1 - core) for by in range(n)]
        return parts[:n], parts[n:]
    parts = pl.pallas_call(
        functools.partial(down_kernel, n),
        grid_spec=pltpu.PrefetchScalarGridSpec(
            num_scalar_prefetch=1,
            grid=(columns // tile,),
            in_specs=[
                pl.BlockSpec((t, rows), lambda i, at: (0, 0)),
                pl.BlockSpec((t, tile), lambda i, at: (0, i)),
            ],
            out_specs=[pl.BlockSpec((rest, tile), lambda i, at: (0, i))] * (2 * n),
            scratch_shapes=[pltpu.VMEM((rows, t), bf16), pltpu.VMEM((rows, tile), bf16)],
        ),
        out_shape=[jax.ShapeDtypeStruct((rest, columns), bf16)] * (2 * n),
        compiler_params=kernel_params(60),
        cost_estimate=kernel_cost(7),
        name="down_product",
    )(jnp.stack([core, me]).astype(jnp.int32), left, right)
    return parts[:n], parts[n:]


def chunks_kernel(transposed, at_ref, x_ref, w_ref, *refs):
    outs, total_ref = refs[:-1], refs[-1]
    t = outs[0].shape[0]
    total_ref[...] = (dot_nt if transposed else dot)(x_ref[...], w_ref[...])
    for k, out_ref in enumerate(outs):
        start = pl.multiple_of(at_ref[k] * t, t)
        out_ref[...] = total_ref[pl.ds(start, t), :].astype(out_ref.dtype)


def chunks_product(x, w, places, transposed):
    rows, depth = x.shape
    n, columns = places.shape[0], w.shape[0 if transposed else 1]
    tile = tile_of(columns)
    w_spec = (
        pl.BlockSpec((tile, depth), lambda i, at: (i, 0))
        if transposed
        else pl.BlockSpec((depth, tile), lambda i, at: (0, i))
    )
    return pl.pallas_call(
        functools.partial(chunks_kernel, transposed),
        grid_spec=pltpu.PrefetchScalarGridSpec(
            num_scalar_prefetch=1,
            grid=(columns // tile,),
            in_specs=[pl.BlockSpec((rows, depth), lambda i, at: (0, 0)), w_spec],
            out_specs=[pl.BlockSpec((rows // n, tile), lambda i, at: (0, i))] * n,
            scratch_shapes=[pltpu.VMEM((rows, tile), f32)],
        ),
        out_shape=[
            jax.ShapeDtypeStruct((rows // n, columns), bf16 if k == 1 % n else f32) for k in range(n)
        ],
        compiler_params=kernel_params(60),
        cost_estimate=kernel_cost(8),
        name="chunks_product",
    )(places, x, w)


def heads_kernel(x_ref, w_ref, out_ref):
    out_ref[0] = dot_nt(x_ref[...], w_ref[...]).astype(bf16)


def heads_product(x, w, n, nz):
    rows, depth = x.shape
    rest, feats = w.shape[0] // (2 * n), w.shape[0] // nz
    per = feats // rest

    def place(i):
        block = i % n * 2 + i // n
        return (block // per, 0, block % per)

    return pl.pallas_call(
        heads_kernel,
        grid=(2 * n,),
        in_specs=[
            pl.BlockSpec((rows, depth), lambda i: (0, 0)),
            pl.BlockSpec((rest, depth), lambda i: (i, 0)),
        ],
        out_specs=pl.BlockSpec((1, rows, rest), place),
        out_shape=jax.ShapeDtypeStruct((nz, rows, feats), bf16),
        compiler_params=kernel_params(60),
        cost_estimate=kernel_cost(0),
        name="heads_product",
    )(x, w)


def rms_parts(values):
    inverse = lax.rsqrt(jnp.mean(values * values, axis=1, keepdims=True) + norm_eps)
    return (values * inverse, inverse)


def norm_back(grad_normed, gain, normed, inverse):
    scaled = grad_normed * gain
    back = inverse * (scaled - normed * jnp.mean(scaled * normed, axis=1, keepdims=True))
    return (back, jnp.sum(grad_normed * normed, axis=0))


def body(
    tokens,
    cotangent,
    lengths,
    norm_attn,
    w_query,
    w_key,
    w_value,
    w_out,
    norm_ffn,
    w_gate,
    w_up,
    w_down,
):
    t, width = tokens.shape
    own_rows, hidden_width = w_gate.shape
    nz = lax.axis_size("z")
    groups = lax.axis_size("p") * 2
    sources = jnp.asarray(ring_sources(nz), jnp.int32)[lax.axis_index("z")]
    feats = width // nz
    block = hidden_width // (groups * nz)
    units = groups * block
    group_rows = nz * own_rows

    n = lax.axis_size("p")
    me, core = lax.axis_index("p"), lax.axis_index("c")
    hops = nz - 1

    inputs = tokens.astype(f32)
    normed_attn, inverse_attn = rms_parts(inputs)
    normed_attn_b = regrouped((normed_attn * norm_attn).astype(bf16), n)

    w_down_here = gather_rows(w_down).reshape(units, width)
    qkv = jnp.concatenate(
        [w.reshape(own_rows, nz, feats) for w in (w_query, w_key, w_value)], axis=2
    ).transpose(1, 0, 2)
    qkv = exchange(qkv)
    w_qkv = gather_rows(qkv).reshape(width, 3 * feats)

    tile = 128 if units % 128 == 0 else units
    cut = -(-units // 256) * 256
    pieces = unit_pieces(n, nz, block, tile)
    gate_up = spread(w_gate, w_up, nz, pieces)
    def laid(whole, part, k):
        return lax.dynamic_update_slice(whole, part, (sources[k] * part.shape[0], 0))

    came, out_came = normed_attn_b, w_out
    attn_in = laid(jnp.zeros((nz * t, width), bf16), came, 0)
    out_rows = laid(jnp.zeros((nz * own_rows, width), bf16), out_came, 0)
    for k in range(hops):
        (came, out_came), (w_down_here, gate_up, attn_in, out_rows) = tick(
            [(hop, came), (hop, out_came)], (w_down_here, gate_up, attn_in, out_rows)
        )
        attn_in, out_rows = laid(attn_in, came, k + 1), laid(out_rows, out_came, k + 1)
    w_out_all = gather_rows(out_rows.reshape(nz, own_rows, width)).reshape(width, width)

    gate_up = exchange(gate_up)
    w_gate_up = gather_rows(gate_up).reshape(width, 2 * units)
    cot = [after(cotangent, gate_up)]

    docs = doc_number(jnp.arange(nz * t, dtype=jnp.int32), jnp.cumsum(lengths[0]))
    docs_down, docs_across = docs[:, None], docs[None, :]
    def cot_hop():
        return [(hop, cot[-1])] if len(cot) < nz else []

    three = dot(attn_in, w_qkv).astype(bf16)
    attended = local_kernel(attention_kernel, feats, three, docs_down, docs_across)
    part, attended = tick(cot_hop(), attended)
    cot += part
    (attended_b,), _ = tick([(exchange, attended.reshape(nz, t, feats))])
    attended_b = regrouped(attended_b.transpose(1, 0, 2).reshape(t, width), n)
    middle = inputs + dot(attended_b, w_out_all)
    normed_ffn, inverse_ffn = rms_parts(middle)
    normed_ffn_b = regrouped((normed_ffn * norm_ffn).astype(bf16), n)
    part, normed_ffn_b = tick(cot_hop(), normed_ffn_b)
    cot += part

    ffn_in = [normed_ffn_b]
    for _ in range(hops):
        (part, *more), _ = tick([(hop, ffn_in[-1])] + cot_hop())
        ffn_in.append(part)
        cot += more

    def ring_first(partials):
        return hop(partials[1 % nz].astype(bf16))

    hidden, grad_gate_up, left, right = feed(ffn_in, cot, sources, w_gate_up, w_down_here, tile)
    line = Line()

    def other_half(x, y):
        return rows_product(x, y, 1 - core, me, n, "other")

    def core_swap(parts):
        return [cross(part, "c", 1) for part in parts]

    def gu_piece(first, last):
        return lambda x, came: rows_product(
            x, grad_gate_up, core, me, n, "cut", came, first, last
        )

    def summed_piece(own, came):
        return line(lambda own, came: summed(own, *came).astype(bf16), own, came)

    def to_line_sum(x):
        return lax.psum_scatter(x, "z", scatter_dimension=0, tiled=True)

    grad_normed_ffn = to_line_sum(line(lambda x: dot_nt(x, w_gate_up).astype(bf16), grad_gate_up))
    gu_other = core_swap(line(other_half, left, grad_gate_up))
    down_own, down_other = line(lambda x, y: down_product(x, y, core, me, n), hidden, right)
    down_other = core_swap(down_other)
    first_own, *first_parts = line(gu_piece(0, cut), left, gu_other)
    first_came = plane_sent(first_parts, 1, n - 1)
    second_own, *second_parts = line(gu_piece(cut, 2 * units), left, gu_other)
    out_parts = line(lambda x: dot(x, w_down_here).astype(bf16), hidden)

    def ffn_back_piece(total):
        total = ungrouped(total.astype(f32), n)
        back, gain_part = norm_back(total, norm_ffn, normed_ffn, inverse_ffn)
        grad_middle = cotangent.astype(f32) + back
        return grad_middle, grad_middle.astype(bf16), gain_part

    grad_normed_ffn, first_came, first_parts = line.hold(grad_normed_ffn, first_came, first_parts)
    first_came = first_came + plane_sent(first_parts, n - 1, n)
    grad_middle, grad_branch_b, gain_ffn_part = line(ffn_back_piece, grad_normed_ffn)
    grad_att = exchange(line(lambda x: heads_product(x, w_out_all, n, nz), grad_branch_b))
    branch = lax.all_gather(grad_branch_b, "z", axis=0, tiled=True)
    down_sums = line(
        lambda own, came: [plus(x, y).astype(bf16) for x, y in zip(own, came, strict=True)][1:],
        down_own,
        down_other,
    )
    first_came, second_parts = line.hold(first_came, second_parts)
    second_came = plane_sent(second_parts, 1, n - 1)
    grad_first = summed_piece(first_own, first_came)
    second_came, second_parts = line.hold(second_came, second_parts)
    second_came = second_came + plane_sent(second_parts, n - 1, n)
    grad_three = line(
        lambda x: local_kernel(
            attention_back_kernel,
            3 * feats,
            three,
            x.reshape(nz * t, feats),
            docs_down,
            docs_across,
        ),
        grad_att,
    )
    grad_first = exchange(grad_first.reshape(nz, own_rows, cut))
    grad_normed_attn = to_line_sum(line(lambda x: dot_nt(x, w_qkv).astype(bf16), grad_three))
    qkv_other = core_swap(line(other_half, attn_in, grad_three))
    second_came = line.hold(second_came)
    qkv_own, *qkv_parts = line(
        lambda x, came: rows_product(x, grad_three, core, me, n, "cut", came), attn_in, qkv_other
    )
    qkv_came = plane_sent(qkv_parts, 1, n - 1)
    qkv_came, qkv_parts = line.hold(qkv_came, qkv_parts)
    qkv_came = qkv_came + plane_sent(qkv_parts, n - 1, n)
    grad_first, out_parts = line.hold(grad_first, out_parts)
    out_total = to_line_sum(out_parts)
    grad_second = summed_piece(second_own, second_came)
    grad_second = exchange(grad_second.reshape(nz, own_rows, 2 * units - cut))
    out_other = core_swap(line(other_half, attended, branch))
    qkv_came, down_sums = line.hold(qkv_came, down_sums)
    out_own, *out_sums = line(
        lambda x, y, came: rows_product(x, y, core, me, n, "cut", came), attended, branch, out_other
    )
    down_came = plane_sent(down_sums, 1, n - 1)
    grad_qkv = summed_piece(qkv_own, qkv_came)
    grad_second = line.hold(grad_second)
    grad_qkv = exchange(grad_qkv.reshape(nz, own_rows, 3 * feats))

    def attn_norm_piece(total):
        total = ungrouped(total.astype(f32), n)
        back, gain_part = norm_back(total, norm_attn, normed_attn, inverse_attn)
        return grad_middle + back, jnp.stack([gain_part, gain_ffn_part])

    token_grad, gains = line(attn_norm_piece, grad_normed_attn)
    out_sums = line.hold(out_sums)
    out_sums = plane_sent(out_sums, 1, n)
    down_came, down_sums = line.hold(down_came, down_sums)
    down_came = down_came + plane_sent(down_sums, n - 1, n)
    grad_w_out = summed_piece(out_own, out_sums)
    grad_w_out = lax.ppermute(
        grad_w_out, ("p", "z"), [(i * nz + j, j * nz + i) for i in range(n) for j in range(nz)]
    )
    grad_w_gate, grad_w_up = line(lambda x, y: collect(x, y, pieces), grad_first, grad_second)

    def three_piece(x):
        return [
            x[:, :, i * feats : (i + 1) * feats]
            .transpose(1, 0, 2)
            .reshape(own_rows, width)
            .astype(f32)
            for i in range(3)
        ]

    grad_w_query, grad_w_key, grad_w_value = line(three_piece, grad_qkv)

    grad_w_down = line(
        lambda own, other, came: summed(plus(own[0], other[0]), *came),
        down_own,
        down_other,
        down_came,
    )
    activations = (middle + out_total.astype(f32)).astype(bf16)
    for axis in ("c", "p", "z"):
        gains = paired_sum([gains, *spread_sums(gains, axis)])
    grad_w_out = line(lambda x: x.astype(f32), grad_w_out)
    gains = gains + jnp.sum(line.token)
    grad_w_down = grad_w_down.astype(f32)
    return (
        activations,
        token_grad,
        gains[0],
        grad_w_query,
        grad_w_key,
        grad_w_value,
        grad_w_out,
        gains[1],
        grad_w_gate,
        grad_w_up,
        grad_w_down,
    )


def solution(mesh):
    dp, seq = mesh.shape["dp"], mesh.shape["seq"]
    grid = Mesh(mesh.devices.reshape(dp // 2, 2, seq), ALL)
    split = P(ALL, None)
    return jax.shard_map(
        body,
        mesh=grid,
        in_specs=(split, split, P(("p", "c"), None), P())
        + (split,) * 4
        + (P(),)
        + (split,) * 3,
        out_specs=(split, split, P(), split, split, split, split, P(), split, split, split),
        check_vma=False,
    )
```

```python
import functools
import math

import jax
import jax.numpy as jnp
from jax import lax
from jax.experimental import pallas as pl
from jax.experimental.pallas import tpu as pltpu
from jax.sharding import Mesh
from jax.sharding import PartitionSpec as P

HEADS = 16
HEAD = 128
WINDOW = 64
BLOCK = 128
PARTS = 1

ALL = ("p", "c", "z")
norm_eps = 1e-05
masked_score = -1e30
f32 = jnp.float32
bf16 = jnp.bfloat16


def dot(left, right, dims=((1,), (0,))):
    return lax.dot_general(left, right, (dims, ((), ())), preferred_element_type=f32)


def dot_nt(left, right):
    return dot(left, right, ((1,), (1,)))


def dot_tn(left, right):
    return dot(left, right, ((0,), (0,)))


def cross(x, axis, by):
    n = lax.axis_size(axis)
    return lax.ppermute(x, axis, [(i, i ^ by) for i in range(n)])


def ring_order(n):
    return list(range(1, n, 2)) + list(range(n - 2, -1, -2)) if n > 1 else [0]


def hop(x):
    n = lax.axis_size("z")
    order = ring_order(n)
    return lax.ppermute(x, "z", [(order[i], order[(i + 1) % n]) for i in range(n)])


def ring_sources(n):
    order = ring_order(n)
    spot = {place: at for at, place in enumerate(order)}
    return [[order[(spot[z] - k) % n] for k in range(n)] for z in range(n)]


def placed(parts, sources):
    out = jnp.zeros((len(parts),) + parts[0].shape, parts[0].dtype)
    for k, part in enumerate(parts):
        out = lax.dynamic_update_slice(out, part[None], (sources[k],) + (0,) * part.ndim)
    return out.reshape((-1,) + parts[0].shape[1:])


def gather_rows(x):
    return lax.all_gather(x, ("c", "p"), axis=0, tiled=False)


def indexed(x, at, axis):
    return lax.dynamic_index_in_dim(x, at, axis, keepdims=False)


def after(x, *others):
    return lax.optimization_barrier((x, others))[0]


def blocks_in_order(x, order):
    wide = x.shape[1] // len(order)
    return jnp.concatenate([x[:, i * wide : (i + 1) * wide] for i in order], axis=1)


def regrouped(x, n):
    return blocks_in_order(x, [2 * i + c for c in range(2) for i in range(n)])


def ungrouped(x, n):
    return blocks_in_order(x, [c * n + i for i in range(n) for c in range(2)])


def tick(jobs, also=()):
    operands = lax.optimization_barrier([operand for _, operand in jobs])
    results = [job(operand) for (job, _), operand in zip(jobs, operands, strict=True)]
    return lax.optimization_barrier((results, also))


def crossing(axis, by):
    return lambda x: cross(x, axis, by)


def exchange(x):
    return lax.all_to_all(x, "z", 0, 0, tiled=True)


def plus(kept, came):
    return kept.astype(f32) + came.astype(f32)


class Line:
    def __init__(self):
        self.token = lax.optimization_barrier(jnp.zeros((8, 128), f32))

    def hold(self, *values):
        values, self.token = lax.optimization_barrier((values, self.token))
        return values[0] if len(values) == 1 else values

    def __call__(self, piece, *values):
        values, self.token = lax.optimization_barrier((values, self.token))
        return self.hold(piece(*values))


def plane_sent(parts, first, last):
    return [cross(parts[by - 1], "p", by) for by in range(first, last)]


def summed(*parts):
    return sum(part.astype(f32) for part in parts)


def spread_sums(x, axis):
    return [cross(x, axis, by) for by in range(1, lax.axis_size(axis))]


def paired_sum(parts):
    while len(parts) > 1:
        parts = [parts[i] + parts[i + 1] for i in range(0, len(parts), 2)]
    return parts[0]


def doc_number(positions, doc_ends):
    return jnp.sum((positions[:, None] >= doc_ends[None, :]).astype(jnp.int32), axis=1)


def allowed_pairs(at, low, count, docs_down_ref, docs_across_ref):
    query_at = at + lax.broadcasted_iota(jnp.int32, (BLOCK, count), 0)
    key_at = low + lax.broadcasted_iota(jnp.int32, (BLOCK, count), 1)
    same = docs_down_ref[at : at + BLOCK, :] == docs_across_ref[:, low : low + count]
    return (key_at <= query_at) & (key_at > query_at - WINDOW) & same


def softmax(query, key, allowed):
    scores = jnp.where(allowed, dot_nt(query, key) * (1.0 / math.sqrt(HEAD)), masked_score)
    exped = jnp.exp(scores - jnp.max(scores, axis=-1, keepdims=True))
    return exped / jnp.sum(exped, axis=-1, keepdims=True)


def attention_kernel(qkv_ref, docs_down_ref, docs_across_ref, out_ref):
    length, width = out_ref.shape
    for at in range(0, length, BLOCK):
        low = max(0, at - BLOCK)
        allowed = allowed_pairs(at, low, at + BLOCK - low, docs_down_ref, docs_across_ref)
        for h in range(0, width, HEAD):
            query = qkv_ref[at : at + BLOCK, h : h + HEAD]
            key = qkv_ref[low : at + BLOCK, width + h : width + h + HEAD]
            value = qkv_ref[low : at + BLOCK, 2 * width + h : 2 * width + h + HEAD]
            probs = softmax(query, key, allowed)
            out_ref[at : at + BLOCK, h : h + HEAD] = dot(probs.astype(bf16), value).astype(bf16)


def attention_back_kernel(qkv_ref, grad_ref, docs_down_ref, docs_across_ref, out_ref):
    length, width = grad_ref.shape
    scale = 1.0 / math.sqrt(HEAD)
    pending = {}
    for at in range(0, length, BLOCK):
        low = max(0, at - BLOCK)
        allowed = allowed_pairs(at, low, at + BLOCK - low, docs_down_ref, docs_across_ref)
        for h in range(0, width, HEAD):
            query = qkv_ref[at : at + BLOCK, h : h + HEAD]
            key = qkv_ref[low : at + BLOCK, width + h : width + h + HEAD]
            value = qkv_ref[low : at + BLOCK, 2 * width + h : 2 * width + h + HEAD]
            grad = grad_ref[at : at + BLOCK, h : h + HEAD]
            probs = softmax(query, key, allowed)
            grad_probs = dot_nt(grad, value)
            inner = jnp.sum(probs * grad_probs, axis=-1, keepdims=True)
            grad_scores = (probs * (grad_probs - inner)).astype(bf16)
            out_ref[at : at + BLOCK, h : h + HEAD] = (dot(grad_scores, key) * scale).astype(bf16)
            grad_key = dot_tn(grad_scores, query) * scale
            grad_value = dot_tn(probs.astype(bf16), grad)
            if at > 0:
                before_key, before_value = pending[h]
                out_ref[low:at, width + h : width + h + HEAD] = (
                    before_key + grad_key[:BLOCK]
                ).astype(bf16)
                out_ref[low:at, 2 * width + h : 2 * width + h + HEAD] = (
                    before_value + grad_value[:BLOCK]
                ).astype(bf16)
            pending[h] = (grad_key[at - low :], grad_value[at - low :])
    for h, (last_key, last_value) in pending.items():
        out_ref[length - BLOCK :, width + h : width + h + HEAD] = last_key.astype(bf16)
        out_ref[length - BLOCK :, 2 * width + h : 2 * width + h + HEAD] = last_value.astype(bf16)


def local_kernel(kernel, columns, *args):
    length = args[0].shape[0]
    return pl.pallas_call(
        kernel,
        out_shape=jax.ShapeDtypeStruct((length, columns), bf16),
        in_specs=[pl.BlockSpec(memory_space=pltpu.VMEM)] * len(args),
        out_specs=pl.BlockSpec(memory_space=pltpu.VMEM),
        compiler_params=kernel_params(10),
        cost_estimate=kernel_cost(0),
    )(*args)


def unit_pieces(n, nz, block, tile):
    pieces = []
    for j in range(2 * n * nz):
        start = ((j // nz % 2) * n + j // nz // 2) * block
        at = start
        while at < start + block:
            end = min(start + block, (at // tile + 1) * tile)
            column = at // tile * 2 * tile + at % tile
            pieces.append((j * block + at - start, j % nz, column, column + tile, end - at))
            at = end
    return pieces


def spread_kernel(pieces, gate_ref, up_ref, out_ref):
    for stored, z, gate_at, up_at, size in pieces:
        out_ref[z, :, gate_at : gate_at + size] = gate_ref[:, stored : stored + size]
        out_ref[z, :, up_at : up_at + size] = up_ref[:, stored : stored + size]


def collect_kernel(pieces, cut, first_ref, second_ref, gate_ref, up_ref):
    for stored, z, gate_at, up_at, size in pieces:
        for at, ref in ((gate_at, gate_ref), (up_at, up_ref)):
            inside = min(max(cut - at, 0), size)
            for source, low, start, count in (
                (first_ref, at, stored, inside),
                (second_ref, at + inside - cut, stored + inside, size - inside),
            ):
                if count:
                    ref[:, start : start + count] = source[z, :, low : low + count].astype(f32)


def spread(gate, up, nz, pieces):
    rows, wide = gate.shape
    return pl.pallas_call(
        functools.partial(spread_kernel, pieces),
        out_shape=jax.ShapeDtypeStruct((nz, rows, 2 * wide // nz), gate.dtype),
        name="spread_units",
    )(gate, up)


def collect(first, second, pieces):
    nz, rows, cut = first.shape
    wide = nz * (cut + second.shape[2]) // 2
    return pl.pallas_call(
        functools.partial(collect_kernel, pieces, cut),
        out_shape=[jax.ShapeDtypeStruct((rows, wide), f32)] * 2,
        name="collect_units",
    )(first, second)


def three_kernel(x_ref, *outs):
    feats = x_ref.shape[2] // 3
    for z in range(x_ref.shape[0]):
        for i, out_ref in enumerate(outs):
            part = x_ref[z, :, i * feats : (i + 1) * feats]
            out_ref[:, z * feats : (z + 1) * feats] = part.astype(f32)


def three_apart(x):
    nz, rows, wide = x.shape
    return pl.pallas_call(
        three_kernel,
        out_shape=[jax.ShapeDtypeStruct((rows, nz * wide // 3), f32)] * 3,
        name="three_apart",
    )(x)


def units_back(gate, up, grad_hidden):
    sig = jax.nn.sigmoid(gate)
    silu = gate * sig
    return (
        (silu * up).astype(bf16),
        (grad_hidden * up * sig * (1.0 + gate * (1.0 - sig))).astype(bf16),
        (grad_hidden * silu).astype(bf16),
    )


def feed_kernel(nz, places_ref, *refs):
    lefts, rights = refs[:nz], refs[nz : 2 * nz]
    gate_up_ref, down_ref, hidden_ref, grad_ref, left_ref, right_ref = refs[2 * nz :]
    t, tile = lefts[0].shape[0], down_ref.shape[0]

    @pl.when(pl.program_id(0) == 0)
    def _():
        for k in range(nz):
            start = pl.multiple_of(places_ref[k] * t, t)
            left_ref[pl.ds(start, t), :] = lefts[k][...]
            right_ref[pl.ds(start, t), :] = rights[k][...]

    both = dot(left_ref[...], gate_up_ref[...])
    grad_hidden = dot_nt(right_ref[...], down_ref[...])
    hidden, grad_gate, grad_up = units_back(both[:, :tile], both[:, tile:], grad_hidden)
    hidden_ref[...] = hidden
    grad_ref[:, :tile] = grad_gate
    grad_ref[:, tile:] = grad_up


def feed(lefts, rights, places, w_gate_up, w_down, tile):
    nz, (t, width) = len(lefts), lefts[0].shape
    units = w_down.shape[0]
    if tile != 128:
        left, right = placed(lefts, places), placed(rights, places)
        both = dot(left, w_gate_up)
        grad_hidden = dot_nt(right, w_down)
        hidden, grad_gate, grad_up = units_back(both[:, :units], both[:, units:], grad_hidden)
        return hidden, jnp.concatenate([grad_gate, grad_up], axis=1), left, right
    rows = nz * t
    whole = pl.BlockSpec((t, width), lambda i, at: (0, 0))
    every = pl.BlockSpec((rows, width), lambda i, at: (0, 0))
    return pl.pallas_call(
        functools.partial(feed_kernel, nz),
        grid_spec=pltpu.PrefetchScalarGridSpec(
            num_scalar_prefetch=1,
            grid=(units // tile,),
            in_specs=[whole] * (2 * nz)
            + [
                pl.BlockSpec((width, 2 * tile), lambda i, at: (0, i)),
                pl.BlockSpec((tile, width), lambda i, at: (i, 0)),
            ],
            out_specs=[
                pl.BlockSpec((rows, tile), lambda i, at: (0, i)),
                pl.BlockSpec((rows, 2 * tile), lambda i, at: (0, i)),
                every,
                every,
            ],
        ),
        out_shape=[
            jax.ShapeDtypeStruct((rows, units), bf16),
            jax.ShapeDtypeStruct((rows, 2 * units), bf16),
            jax.ShapeDtypeStruct((rows, width), bf16),
            jax.ShapeDtypeStruct((rows, width), bf16),
        ],
        compiler_params=kernel_params(60),
        cost_estimate=kernel_cost(18),
        name="feed_units",
    )(places, *lefts, *rights, w_gate_up, w_down)


def kernel_cost(us):
    return pl.CostEstimate(flops=int(us * 1.15e9 * 0.5), bytes_accessed=0, transcendentals=0)


def kernel_params(mib):
    return pltpu.CompilerParams(vmem_limit_bytes=mib * 1024 * 1024)


def tile_of(columns, most=1408):
    return max(tile for tile in range(128, most + 1, 128) if columns % tile == 0)


def rows_kernel(n, mode, at_ref, left_ref, right_ref, *refs):
    flip_ref, total_ref = refs[-2:]
    came, outs = (refs[:0], refs[:-2]) if mode == "other" else (refs[:PARTS], refs[PARTS:-2])

    @pl.when(pl.program_id(0) == 0)
    def _():
        flip_ref[...] = left_ref[...].T

    total = dot(flip_ref[...], right_ref[...])
    size = total.shape[0] // PARTS
    for k in range(PARTS):
        part = total[k * size : (k + 1) * size]
        if mode == "other":
            outs[k][...] = part.astype(bf16)
        else:
            part = (part + came[k][...].astype(f32)).astype(bf16)
            into = outs[0] if mode == "whole" else total_ref
            into[k * size : (k + 1) * size, :] = part
    if mode == "cut":
        rest = total.shape[0] // n
        for by in range(n):
            start = pl.multiple_of((at_ref[1] ^ by) * rest, rest)
            outs[by][...] = total_ref[pl.ds(start, rest), :]


def rows_product(left, right, half, me, n, mode, came=(), first=0, last=None):
    t, rows = left.shape[0], left.shape[1] // 2
    last = right.shape[1] if last is None else last
    tile = tile_of(math.gcd(last - first, first) if first else last)
    rest, columns, off = rows // n, last - first, first // tile
    at = jnp.stack([half, me]).astype(jnp.int32)
    outs, height = {"whole": (1, rows), "cut": (n, rest), "other": (PARTS, rows // PARTS)}[mode]
    return pl.pallas_call(
        functools.partial(rows_kernel, n, mode),
        grid_spec=pltpu.PrefetchScalarGridSpec(
            num_scalar_prefetch=1,
            grid=(columns // tile,),
            in_specs=[
                pl.BlockSpec((t, rows), lambda i, at: (0, at[0])),
                pl.BlockSpec((t, tile), lambda i, at: (0, i + off)),
            ]
            + [pl.BlockSpec((rows // PARTS, tile), lambda i, at: (0, i + off))] * len(came),
            out_specs=[pl.BlockSpec((height, tile), lambda i, at: (0, i))] * outs,
            scratch_shapes=[pltpu.VMEM((rows, t), bf16), pltpu.VMEM((rows, tile), bf16)],
        ),
        out_shape=[jax.ShapeDtypeStruct((height, columns), bf16)] * outs,
        compiler_params=kernel_params(60),
        cost_estimate=kernel_cost(6.5),
        name="rows_product",
    )(at, left, right, *came)


def down_kernel(n, at_ref, left_ref, right_ref, *refs):
    outs, flip_ref, total_ref = refs[:-2], refs[-2], refs[-1]
    rest = outs[0].shape[0]

    @pl.when(pl.program_id(0) == 0)
    def _():
        flip_ref[...] = left_ref[...].T

    total_ref[...] = dot(flip_ref[...], right_ref[...]).astype(bf16)
    for k, out_ref in enumerate(outs):
        half = at_ref[0] if k < n else 1 - at_ref[0]
        start = (half * n + (at_ref[1] ^ (k % n))) * rest
        out_ref[...] = total_ref[pl.ds(pl.multiple_of(start, math.gcd(rest, 16)), rest), :]


def down_product(left, right, core, me, n):
    t, rows = left.shape
    columns = right.shape[1]
    tile = tile_of(columns)
    rest = rows // (2 * n)
    if rest % 16:
        full = dot_tn(left, right).astype(bf16).reshape(2, n, rest, columns)
        parts = [indexed(indexed(full, at, 0), me ^ by, 0) for at in (core, 1 - core) for by in range(n)]
        return parts[:n], parts[n:]
    parts = pl.pallas_call(
        functools.partial(down_kernel, n),
        grid_spec=pltpu.PrefetchScalarGridSpec(
            num_scalar_prefetch=1,
            grid=(columns // tile,),
            in_specs=[
                pl.BlockSpec((t, rows), lambda i, at: (0, 0)),
                pl.BlockSpec((t, tile), lambda i, at: (0, i)),
            ],
            out_specs=[pl.BlockSpec((rest, tile), lambda i, at: (0, i))] * (2 * n),
            scratch_shapes=[pltpu.VMEM((rows, t), bf16), pltpu.VMEM((rows, tile), bf16)],
        ),
        out_shape=[jax.ShapeDtypeStruct((rest, columns), bf16)] * (2 * n),
        compiler_params=kernel_params(60),
        cost_estimate=kernel_cost(7),
        name="down_product",
    )(jnp.stack([core, me]).astype(jnp.int32), left, right)
    return parts[:n], parts[n:]


def chunks_kernel(transposed, at_ref, x_ref, w_ref, *refs):
    outs, total_ref = refs[:-1], refs[-1]
    t = outs[0].shape[0]
    total_ref[...] = (dot_nt if transposed else dot)(x_ref[...], w_ref[...])
    for k, out_ref in enumerate(outs):
        start = pl.multiple_of(at_ref[k] * t, t)
        out_ref[...] = total_ref[pl.ds(start, t), :].astype(out_ref.dtype)


def chunks_product(x, w, places, transposed):
    rows, depth = x.shape
    n, columns = places.shape[0], w.shape[0 if transposed else 1]
    tile = tile_of(columns)
    w_spec = (
        pl.BlockSpec((tile, depth), lambda i, at: (i, 0))
        if transposed
        else pl.BlockSpec((depth, tile), lambda i, at: (0, i))
    )
    return pl.pallas_call(
        functools.partial(chunks_kernel, transposed),
        grid_spec=pltpu.PrefetchScalarGridSpec(
            num_scalar_prefetch=1,
            grid=(columns // tile,),
            in_specs=[pl.BlockSpec((rows, depth), lambda i, at: (0, 0)), w_spec],
            out_specs=[pl.BlockSpec((rows // n, tile), lambda i, at: (0, i))] * n,
            scratch_shapes=[pltpu.VMEM((rows, tile), f32)],
        ),
        out_shape=[
            jax.ShapeDtypeStruct((rows // n, columns), bf16 if k == 1 % n else f32) for k in range(n)
        ],
        compiler_params=kernel_params(60),
        cost_estimate=kernel_cost(8),
        name="chunks_product",
    )(places, x, w)


def heads_kernel(x_ref, w_ref, out_ref):
    out_ref[0] = dot_nt(x_ref[...], w_ref[...]).astype(bf16)


def heads_product(x, w, n, nz):
    rows, depth = x.shape
    rest, feats = w.shape[0] // (2 * n), w.shape[0] // nz
    per = feats // rest

    def place(i):
        block = i % n * 2 + i // n
        return (block // per, 0, block % per)

    return pl.pallas_call(
        heads_kernel,
        grid=(2 * n,),
        in_specs=[
            pl.BlockSpec((rows, depth), lambda i: (0, 0)),
            pl.BlockSpec((rest, depth), lambda i: (i, 0)),
        ],
        out_specs=pl.BlockSpec((1, rows, rest), place),
        out_shape=jax.ShapeDtypeStruct((nz, rows, feats), bf16),
        compiler_params=kernel_params(60),
        cost_estimate=kernel_cost(0),
        name="heads_product",
    )(x, w)


def rms_parts(values):
    inverse = lax.rsqrt(jnp.mean(values * values, axis=1, keepdims=True) + norm_eps)
    return (values * inverse, inverse)


def norm_back(grad_normed, gain, normed, inverse):
    scaled = grad_normed * gain
    back = inverse * (scaled - normed * jnp.mean(scaled * normed, axis=1, keepdims=True))
    return (back, jnp.sum(grad_normed * normed, axis=0))


def body(
    tokens,
    cotangent,
    lengths,
    norm_attn,
    w_query,
    w_key,
    w_value,
    w_out,
    norm_ffn,
    w_gate,
    w_up,
    w_down,
):
    t, width = tokens.shape
    own_rows, hidden_width = w_gate.shape
    nz = lax.axis_size("z")
    groups = lax.axis_size("p") * 2
    sources = jnp.asarray(ring_sources(nz), jnp.int32)[lax.axis_index("z")]
    feats = width // nz
    block = hidden_width // (groups * nz)
    units = groups * block
    group_rows = nz * own_rows

    n = lax.axis_size("p")
    me, core = lax.axis_index("p"), lax.axis_index("c")
    hops = nz - 1

    inputs = tokens.astype(f32)
    normed_attn, inverse_attn = rms_parts(inputs)
    normed_attn_b = regrouped((normed_attn * norm_attn).astype(bf16), n)

    w_down_here = gather_rows(w_down).reshape(units, width)
    qkv = jnp.concatenate(
        [w.reshape(own_rows, nz, feats) for w in (w_query, w_key, w_value)], axis=2
    ).transpose(1, 0, 2)
    qkv = exchange(qkv)
    w_qkv = gather_rows(qkv).reshape(width, 3 * feats)

    tile = 128 if units % 128 == 0 else units
    cut = -(-units // 256) * 256
    pieces = unit_pieces(n, nz, block, tile)
    gate_up = spread(w_gate, w_up, nz, pieces)
    def laid(whole, part, k):
        return lax.dynamic_update_slice(whole, part, (sources[k] * part.shape[0], 0))

    came, out_came = normed_attn_b, w_out
    attn_in = laid(jnp.zeros((nz * t, width), bf16), came, 0)
    out_rows = laid(jnp.zeros((nz * own_rows, width), bf16), out_came, 0)
    for k in range(hops):
        (came, out_came), (w_down_here, gate_up, attn_in, out_rows) = tick(
            [(hop, came), (hop, out_came)], (w_down_here, gate_up, attn_in, out_rows)
        )
        attn_in, out_rows = laid(attn_in, came, k + 1), laid(out_rows, out_came, k + 1)
    w_out_all = gather_rows(out_rows.reshape(nz, own_rows, width)).reshape(width, width)

    gate_up = exchange(gate_up)
    w_gate_up = gather_rows(gate_up).reshape(width, 2 * units)
    cot = [after(cotangent, gate_up)]

    docs = doc_number(jnp.arange(nz * t, dtype=jnp.int32), jnp.cumsum(lengths[0]))
    docs_down, docs_across = docs[:, None], docs[None, :]
    def cot_hop():
        return [(hop, cot[-1])] if len(cot) < nz else []

    three = dot(attn_in, w_qkv).astype(bf16)
    attended = local_kernel(attention_kernel, feats, three, docs_down, docs_across)
    part, attended = tick(cot_hop(), attended)
    cot += part
    (attended_b,), _ = tick([(exchange, attended.reshape(nz, t, feats))])
    attended_b = regrouped(attended_b.transpose(1, 0, 2).reshape(t, width), n)
    middle = inputs + dot(attended_b, w_out_all)
    normed_ffn, inverse_ffn = rms_parts(middle)
    normed_ffn_b = regrouped((normed_ffn * norm_ffn).astype(bf16), n)
    part, normed_ffn_b = tick(cot_hop(), normed_ffn_b)
    cot += part

    ffn_in = [normed_ffn_b]
    for _ in range(hops):
        (part, *more), _ = tick([(hop, ffn_in[-1])] + cot_hop())
        ffn_in.append(part)
        cot += more

    def ring_first(partials):
        return hop(partials[1 % nz].astype(bf16))

    hidden, grad_gate_up, left, right = feed(ffn_in, cot, sources, w_gate_up, w_down_here, tile)
    line = Line()

    def other_half(x, y):
        return rows_product(x, y, 1 - core, me, n, "other")

    def core_swap(parts):
        return [cross(part, "c", 1) for part in parts]

    def gu_piece(first, last):
        return lambda x, came: rows_product(
            x, grad_gate_up, core, me, n, "cut", came, first, last
        )

    def summed_piece(own, came):
        return line(lambda own, came: summed(own, *came).astype(bf16), own, came)

    def to_line_sum(x):
        return lax.psum_scatter(x, "z", scatter_dimension=0, tiled=True)

    grad_normed_ffn = to_line_sum(line(lambda x: dot_nt(x, w_gate_up).astype(bf16), grad_gate_up))
    gu_other = core_swap(line(other_half, left, grad_gate_up))
    down_own, down_other = line(lambda x, y: down_product(x, y, core, me, n), hidden, right)
    down_other = core_swap(down_other)
    first_own, *first_parts = line(gu_piece(0, cut), left, gu_other)
    first_came = plane_sent(first_parts, 1, n - 1)
    second_own, *second_parts = line(gu_piece(cut, 2 * units), left, gu_other)
    out_parts = line(lambda x: dot(x, w_down_here).astype(bf16), hidden)

    def ffn_back_piece(total):
        total = ungrouped(total.astype(f32), n)
        back, gain_part = norm_back(total, norm_ffn, normed_ffn, inverse_ffn)
        grad_middle = cotangent.astype(f32) + back
        return grad_middle, grad_middle.astype(bf16), gain_part

    grad_normed_ffn, first_came, first_parts = line.hold(grad_normed_ffn, first_came, first_parts)
    first_came = first_came + plane_sent(first_parts, n - 1, n)
    grad_middle, grad_branch_b, gain_ffn_part = line(ffn_back_piece, grad_normed_ffn)
    grad_att = exchange(line(lambda x: heads_product(x, w_out_all, n, nz), grad_branch_b))
    branch = lax.all_gather(grad_branch_b, "z", axis=0, tiled=True)
    down_sums = line(
        lambda own, came: [plus(x, y).astype(bf16) for x, y in zip(own, came, strict=True)][1:],
        down_own,
        down_other,
    )
    first_came, second_parts = line.hold(first_came, second_parts)
    second_came = plane_sent(second_parts, 1, n - 1)
    grad_first = summed_piece(first_own, first_came)
    second_came, second_parts = line.hold(second_came, second_parts)
    second_came = second_came + plane_sent(second_parts, n - 1, n)
    grad_three = line(
        lambda x: local_kernel(
            attention_back_kernel,
            3 * feats,
            three,
            x.reshape(nz * t, feats),
            docs_down,
            docs_across,
        ),
        grad_att,
    )
    grad_first = exchange(grad_first.reshape(nz, own_rows, cut))
    grad_normed_attn = to_line_sum(line(lambda x: dot_nt(x, w_qkv).astype(bf16), grad_three))
    qkv_other = core_swap(line(other_half, attn_in, grad_three))
    second_came = line.hold(second_came)
    qkv_own, *qkv_parts = line(
        lambda x, came: rows_product(x, grad_three, core, me, n, "cut", came), attn_in, qkv_other
    )
    qkv_came = plane_sent(qkv_parts, 1, n - 1)
    qkv_came, qkv_parts = line.hold(qkv_came, qkv_parts)
    qkv_came = qkv_came + plane_sent(qkv_parts, n - 1, n)
    grad_first, out_parts = line.hold(grad_first, out_parts)
    out_total = to_line_sum(out_parts)
    grad_second = summed_piece(second_own, second_came)
    grad_second = exchange(grad_second.reshape(nz, own_rows, 2 * units - cut))
    out_other = core_swap(line(other_half, attended, branch))
    qkv_came, down_sums = line.hold(qkv_came, down_sums)
    out_own, *out_sums = line(
        lambda x, y, came: rows_product(x, y, core, me, n, "cut", came), attended, branch, out_other
    )
    down_came = plane_sent(down_sums, 1, n - 1)
    grad_qkv = summed_piece(qkv_own, qkv_came)
    grad_second = line.hold(grad_second)
    grad_qkv = exchange(grad_qkv.reshape(nz, own_rows, 3 * feats))

    def attn_norm_piece(total):
        total = ungrouped(total.astype(f32), n)
        back, gain_part = norm_back(total, norm_attn, normed_attn, inverse_attn)
        return grad_middle + back, jnp.stack([gain_part, gain_ffn_part])

    token_grad, gains = line(attn_norm_piece, grad_normed_attn)
    out_sums = line.hold(out_sums)
    out_sums = plane_sent(out_sums, 1, n)
    down_came, down_sums = line.hold(down_came, down_sums)
    down_came = down_came + plane_sent(down_sums, n - 1, n)
    grad_w_out = summed_piece(out_own, out_sums)
    grad_w_out = lax.ppermute(
        grad_w_out, ("p", "z"), [(i * nz + j, j * nz + i) for i in range(n) for j in range(nz)]
    )
    grad_w_gate, grad_w_up = line(lambda x, y: collect(x, y, pieces), grad_first, grad_second)

    grad_w_query, grad_w_key, grad_w_value = line(three_apart, grad_qkv)

    grad_w_down = line(
        lambda own, other, came: summed(plus(own[0], other[0]), *came),
        down_own,
        down_other,
        down_came,
    )
    activations = (middle + out_total.astype(f32)).astype(bf16)
    for axis in ("c", "p", "z"):
        gains = paired_sum([gains, *spread_sums(gains, axis)])
    grad_w_out = line(lambda x: x.astype(f32), grad_w_out)
    gains = gains + line.token[0, 0]
    grad_w_down = grad_w_down.astype(f32)
    return (
        activations,
        token_grad,
        gains[0],
        grad_w_query,
        grad_w_key,
        grad_w_value,
        grad_w_out,
        gains[1],
        grad_w_gate,
        grad_w_up,
        grad_w_down,
    )


def solution(mesh):
    dp, seq = mesh.shape["dp"], mesh.shape["seq"]
    grid = Mesh(mesh.devices.reshape(dp // 2, 2, seq), ALL)
    split = P(ALL, None)
    return jax.shard_map(
        body,
        mesh=grid,
        in_specs=(split, split, P(("p", "c"), None), P())
        + (split,) * 4
        + (P(),)
        + (split,) * 3,
        out_specs=(split, split, P(), split, split, split, split, P(), split, split, split),
        check_vma=False,
    )
```
